256 devices in a mesh: leaf: 8 (over z), row: 4 (over y), col: 8 (over x, core).
Axes of the slice: x: 4, y: 4, z: 8, core: 2. Of those that a mesh axis runs over, the one named last changes fastest.
Arguments:
- rhs_child: bfloat16 [8, 128, 6144], P('leaf', None, 'col'), may hold values from -6 to 6
- rhs_root: float32 [128, 12288], P(None, 'col'), may hold values from -6 to 6
- fwd_child: bfloat16 [8, 6144, 6144], P('leaf', 'col', 'row'), may hold values from -0.078125 to 0.078125
- coupling: bfloat16 [8, 6144, 4096], P('leaf', 'row', 'col'), may hold values from -0.078125 to 0.078125
- root_inverse: bfloat16 [12288, 12288], P('col', ('leaf', 'row')), may hold values from -0.0546875 to 0.0546875
- back_child: bfloat16 [8, 4096, 6144], P('leaf', None, ('row', 'col')), may hold values from -0.09375 to 0.09375
- bwd_child: bfloat16 [8, 6144, 6144], P('leaf', ('row', 'col')), may hold values from -0.078125 to 0.078125
- parent_rows: int32 [8, 4096], P('leaf'), may hold values from 0 to 12287, as said below
Outputs:
- x_root: float32 [128, 12288], P(None, ('leaf', 'row', 'col'))
- x_child: float32 [8, 128, 6144], P('leaf', None, ('row', 'col'))
The draws below stay inside these ranges and needn't reach their ends.
Inputs may be any that keep to these rules, and one draw needn't show every extreme that they name: For each child, the entries parent_rows[c, q * 512 + i] for 0 <= i < 512 are distinct and lie in q * 1536 to (q + 1) * 1536 - 1.
All inputs are finite; a program needn't handle non-finite values.
Results may differ from the reference program's by a relative error of at most 0.009.
Values may be sent and summed in bfloat16 or wider, within the bound.
A program may use at most 64 MiB of HBM per device.

```python
import jax
import jax.numpy as jnp
from jax import lax

K = 128
S = 6144
R = 4096
P_SIZE = 12288
CHILDREN = 8
PB = 1536
RB = 512


def draw_parent_rows(key, part):
    key = jax.random.fold_in(key, 7)
    blocks = R // RB
    count = CHILDREN * blocks
    scores = jax.random.randint(key, (count, PB), 0, 1 << 20, dtype=jnp.int32)
    scores = scores * PB + jnp.arange(PB, dtype=jnp.int32)[None, :]
    ends = (jnp.arange(PB, dtype=jnp.int32) == 0) | (jnp.arange(PB, dtype=jnp.int32) == PB - 1)
    scores = jnp.where(ends[None, :], -1 - jnp.arange(PB, dtype=jnp.int32)[None, :], scores)
    order = jnp.argsort(scores, axis=1, stable=True).astype(jnp.int32)
    picked = order[:, :RB]
    second = jax.random.fold_in(key, 11)
    mix = jax.random.randint(second, (count, RB), 0, 1 << 20, dtype=jnp.int32) * RB + jnp.arange(RB, dtype=jnp.int32)[None, :]
    shuffle = jnp.argsort(mix, axis=1, stable=True).astype(jnp.int32)
    picked = jnp.take_along_axis(picked, shuffle, axis=1)
    picks = picked.reshape(CHILDREN, blocks, RB)
    offsets = (jnp.arange(blocks, dtype=jnp.int32) * PB)[None, :, None]
    return (picks + offsets).reshape(CHILDREN, R).astype(jnp.int32)


def level_of(key, extent, split, least, high):
    gain, own = 1.0, jax.random.fold_in(key, 6)
    for axis_at, parts in split:
        draws = jnp.exp(jax.random.uniform(jax.random.fold_in(own, axis_at), (parts,), jnp.float32, least / len(split), high / len(split)))
        gain = gain * jnp.repeat(draws, extent[axis_at] // parts).reshape([-1 if axis == axis_at else 1 for axis in range(len(extent))])
    return gain


def noise(own_key, shape, spread, bound, pieces=(), kind=jnp.bfloat16):
    level = level_of(own_key, shape, pieces, -0.22, 0.18) if pieces else 1.0
    values = jax.random.normal(own_key, shape, jnp.float32) * spread * level
    return jnp.minimum(jnp.maximum(values, -bound), bound).astype(kind)


def setup_inputs(seed: int = 0) -> dict:
    splits = jax.random.split(jax.random.key(seed), 9)
    return {
        "rhs_child": noise(splits[0], (CHILDREN, K, S), 1.0, 6.0, ((0, 8), (2, 8))),
        "rhs_root": noise(splits[1], (K, P_SIZE), 1.0, 6.0, ((1, 8),), jnp.float32),
        "fwd_child": noise(splits[2], (CHILDREN, S, S), S ** -0.5, 0.078125, ((0, 8), (1, 8), (2, 4))),
        "coupling": noise(splits[3], (CHILDREN, S, R), S ** -0.5, 0.078125, ((0, 8), (1, 4), (2, 8))),
        "root_inverse": noise(splits[4], (P_SIZE, P_SIZE), P_SIZE ** -0.5, 0.0546875, ((0, 8), (1, 32))),
        "back_child": noise(splits[5], (CHILDREN, R, S), R ** -0.5, 0.09375, ((0, 8), (2, 32))),
        "bwd_child": noise(splits[6], (CHILDREN, S, S), S ** -0.5, 0.078125, ((0, 8), (1, 32))),
        "parent_rows": draw_parent_rows(jax.random.fold_in(splits[8], 71), 0),
    }


def product(left, right):
    return jnp.dot(left.astype(jnp.float32), right.astype(jnp.float32), precision=lax.Precision.HIGHEST, preferred_element_type=jnp.float32)


def reference(rhs_child, rhs_root, fwd_child, coupling, root_inverse, back_child, bwd_child, parent_rows):
    assembled = jnp.zeros(rhs_root.shape, jnp.float32)
    child_list = []
    for child in range(CHILDREN):
        child_y = product(rhs_child[child], fwd_child[child])
        child_list.append(child_y)
        update = product(child_y.astype(jnp.bfloat16), coupling[child])
        assembled = assembled.at[:, parent_rows[child]].add(update)
    parent_rhs = (rhs_root - assembled).astype(jnp.bfloat16)
    x_root = product(parent_rhs, root_inverse)
    root_b = x_root.astype(jnp.bfloat16)
    results = []
    for child in range(CHILDREN):
        selected = jnp.take(root_b, parent_rows[child], axis=1)
        correction = product(selected, back_child[child])
        reduced = (child_list[child] - correction).astype(jnp.bfloat16)
        results.append(product(reduced, bwd_child[child]))
    return x_root, jnp.stack(results)
```

```python
import jax
import jax.numpy as jnp
from jax import lax
from jax.experimental import pallas as pl
from jax.experimental.pallas import tpu as pltpu
from jax.sharding import PartitionSpec as P

BF = jnp.bfloat16
F32 = jnp.float32
MESH = pl.DeviceIdType.MESH
CONTRACT_LAST = (((1,), (1,)), ((), ()))

X_ORDER = (2, 1, 3)
Y_ORDER = (2, 1, 3)
Z_ORDER = (4, 3, 5, 2, 6, 1, 7)
Z_ARRIVAL = (1, 7, 2, 6, 3, 5, 4)
PLANE = sorted(
    ((dy, dx) for dy in range(4) for dx in range(4) if (dy, dx) != (0, 0)),
    key=lambda p: -(min(p[0], 4 - p[0]) + min(p[1], 4 - p[1])),
)
COL = [(dx, dh) for dx in (2, 1, 3) for dh in (1, 0)] + [(0, 1)]


def dot(a, b):
    return jnp.dot(a, b, preferred_element_type=F32)


def dot_last(a, b):
    return lax.dot_general(a, b, CONTRACT_LAST, preferred_element_type=F32)


def kernel(
    rhs_ref, root_ref, fwd_ref, coup_ref, rinv_ref, back_ref, bwd_ref, rows_ref,
    xroot_ref, xchild_ref,
    rhs_v, fwd_v, coup_v, rinv_v, back_v, bwd_v, root_v, rows_v,
    part_f, part_b, core_in, x_out, x_in, y_keep, y_all,
    u_f, u_b, u_in, u_all, place, pick, p_rhs,
    xp_f, xp_b, xp_in, xr_all, rb_all, sel_out, sel_in, sel_all,
    z_out, z_in, zsum, flip,
    load_sem, core_s, core_r, xs_s, xs_r, ag_s, ag_r, fw_s, fw_r,
    us_s, us_r, za_s, za_r, pr_s, pr_r, ya_s, ya_r, xc_s, xc_r, xo_s, xo_r,
    rb_s, rb_r, se_s, se_r, pl_s, pl_r, fin_s, fin_r, end_s, end_r, w_s, w_r,
):
    l, r, q = lax.axis_index("leaf"), lax.axis_index("row"), lax.axis_index("col")
    x, h = q // 2, q % 2
    sib = (l, r, x * 2 + 1 - h)

    def xat(d):
        return lax.rem(x + d, 4)

    def yat(d):
        return lax.rem(r + d, 4)

    def zat(d):
        return lax.rem(l + d, 8)

    def load(src, dst, k):
        c = pltpu.make_async_copy(src, dst, load_sem.at[k])
        c.start()
        return c

    pending = []

    def send(src, dst, ss, rs, device):
        c = pltpu.make_async_remote_copy(
            src_ref=src, dst_ref=dst, send_sem=ss, recv_sem=rs, device_id=device, device_id_type=MESH
        )
        c.start()
        pending.append(c)

    def arrive(dst, ss, rs):
        pltpu.make_async_remote_copy(
            src_ref=dst, dst_ref=dst, send_sem=ss, recv_sem=rs, device_id=sib, device_id_type=MESH
        ).wait_recv()

    def flush():
        while pending:
            pending.pop(0).wait_send()

    partners = [(l, r, xat(dx) * 2 + lax.rem(h + dh, 2)) for dx, dh in COL]
    partners += [(l, yat(dy), xat(dx) * 2 + h) for dy, dx in PLANE if dy]
    partners += [(zat(d), r, q) for d in Z_ORDER]
    bar = pltpu.get_barrier_semaphore()
    for p in partners:
        pl.semaphore_signal(bar, inc=1, device_id=p, device_id_type=MESH)

    l_rhs = load(rhs_ref, rhs_v, 0)
    l_fwd = []
    for j, d in enumerate(X_ORDER + (0,)):
        cols = pl.ds(pl.multiple_of(xat(d) * 384, 128), 384)
        l_fwd.append(load(fwd_ref.at[:, cols], fwd_v.at[j], 1 + j))
    l_rows = load(rows_ref, rows_v.at[l], 5)
    l_coup = load(coup_ref, coup_v, 6)
    l_root = load(root_ref.at[pl.ds(pl.multiple_of(r * 32, 32), 32)], root_v, 7)
    l_rinv = load(rinv_ref, rinv_v, 8)
    l_back = load(back_ref, back_v.at[h], 9)
    l_bwd = load(bwd_ref, bwd_v.at[h], 10)

    mine = pl.ds(pl.multiple_of(h * 64, 64), 64)
    other = pl.ds(pl.multiple_of((1 - h) * 64, 64), 64)
    l_rhs.wait()
    for j in range(4):
        l_fwd[j].wait()
        value = dot(rhs_v[...], fwd_v[j])
        part_f[j] = value
        part_b[j] = value.astype(BF)
        if j == 0:
            pl.semaphore_wait(bar, len(partners))
        send(part_b.at[j, other], core_in.at[j], core_s.at[j], core_r.at[j], sib)
    for j, d in enumerate(X_ORDER + (0,)):
        arrive(core_in.at[j], core_s.at[j], core_r.at[j])
        both = part_f[j, mine, :] + core_in[j].astype(F32)
        if d:
            x_out[j] = both.astype(BF)
            send(x_out.at[j], x_in.at[j], xs_s.at[j], xs_r.at[j], (l, r, xat(d) * 2 + h))
        else:
            y_keep[...] = both

    l_rows.wait()
    for j, d in enumerate(Z_ORDER):
        send(rows_ref, rows_v.at[l], pr_s.at[j], pr_r.at[j], (zat(d), r, q))

    def build_place(leaf):
        row = rows_v[leaf, :, pl.ds(pl.multiple_of(q * 512, 512), 512)] - q * 1536

        @pl.loop(0, 12)
        def _(t):
            at = lax.broadcasted_iota(jnp.int32, (128, 512), 0) + t * 128
            place[leaf, pl.ds(pl.multiple_of(t * 128, 128), 128), :] = (at == row).astype(F32).astype(BF)

    def build_pick(leaf):
        row = rows_v[leaf, :, pl.ds(pl.multiple_of(l * 512 + r * 128, 128), 128)] - l * 1536

        @pl.loop(0, 12)
        def _(t):
            at = lax.broadcasted_iota(jnp.int32, (128, 128), 0) + t * 128
            pick[leaf, pl.ds(pl.multiple_of(t * 128, 128), 128), :] = (at == row).astype(F32).astype(BF)

    def rows_arrive(d):
        j = Z_ORDER.index((8 - d) % 8)
        arrive(rows_v.at[zat(d)], pr_s.at[j], pr_r.at[j])

    build_place(l)
    build_pick(l)
    for d in Z_ARRIVAL[:3]:
        rows_arrive(d)
        build_place(zat(d))
        build_pick(zat(d))

    total = y_keep[...]
    for j in range(3):
        arrive(x_in.at[j], xs_s.at[j], xs_r.at[j])
        total = total + x_in[j].astype(F32)
    y_keep[...] = total
    y_all[x, mine, :] = total.astype(BF)
    for j, d in enumerate(X_ORDER):
        send(y_all.at[x, mine], y_all.at[x, mine], ag_s.at[j], ag_r.at[j], (l, r, xat(d) * 2 + h))
    send(y_all.at[x, mine], y_all.at[x, mine], fw_s.at[3], fw_r.at[3], sib)
    for d in Z_ARRIVAL[3:]:
        rows_arrive(d)
        build_place(zat(d))
        build_pick(zat(d))
    l_coup.wait()
    for d in (1, 3, 2):
        j = X_ORDER.index((4 - d) % 4)
        src = xat(d)
        arrive(y_all.at[src, mine], ag_s.at[j], ag_r.at[j])
        send(y_all.at[src, mine], y_all.at[src, mine], fw_s.at[j], fw_r.at[j], sib)
    update = jnp.zeros((128, 512), F32)
    for d in (0, 1, 3, 2):
        j = X_ORDER.index((4 - d) % 4) if d else 3
        src = xat(d)
        arrive(y_all.at[src, other], fw_s.at[j], fw_r.at[j])
        update = update + dot(y_all[src], coup_v[pl.ds(pl.multiple_of(src * 384, 128), 384), :])

    u_f[...] = update
    u_b[...] = update.astype(BF)
    for j, d in enumerate(Y_ORDER):
        k = pl.ds(pl.multiple_of(yat(d) * 32, 32), 32)
        send(u_b.at[k], u_in.at[j], us_s.at[j], us_r.at[j], (l, yat(d), q))
    flush_before = list(pending)
    pending.clear()
    for c in flush_before[:-3]:
        c.wait_send()
    pending.extend(flush_before[-3:])
    l_back.wait()
    l_bwd.wait()
    send(back_v.at[h], back_v.at[h], w_s.at[0], w_r.at[0], sib)
    send(bwd_v.at[h], bwd_v.at[h], w_s.at[1], w_r.at[1], sib)
    my_k = pl.ds(pl.multiple_of(r * 32, 32), 32)
    total = u_f[my_k, :]
    for j in range(3):
        arrive(u_in.at[j], us_s.at[j], us_r.at[j])
        total = total + u_in[j].astype(F32)
    u_all[l] = total.astype(BF)

    for j, d in enumerate(Z_ORDER):
        send(u_all.at[l], u_all.at[l], za_s.at[j], za_r.at[j], (zat(d), r, q))
    l_root.wait()
    placed = dot_last(u_all[l], place[l])
    for d in Z_ARRIVAL:
        j = Z_ORDER.index((8 - d) % 8)
        leaf = zat(d)
        arrive(u_all.at[leaf], za_s.at[j], za_r.at[j])
        placed = placed + dot_last(u_all[leaf], place[leaf])
    p_rhs[my_k, :] = (root_v[...] - placed).astype(BF)

    for j, d in enumerate(Y_ORDER):
        send(p_rhs.at[my_k], p_rhs.at[my_k], ya_s.at[j], ya_r.at[j], (l, yat(d), q))
    l_rinv.wait()
    for j, d in enumerate(Y_ORDER):
        k = pl.ds(pl.multiple_of(yat(4 - d) * 32, 32), 32)
        arrive(p_rhs.at[k], ya_s.at[j], ya_r.at[j])
    value = dot(p_rhs[...], rinv_v[...])

    xp_f[...] = value
    xp_b[...] = value.astype(BF)
    for j, (dx, dh) in enumerate(COL):
        tx, th = xat(dx), lax.rem(h + dh, 2)
        k = pl.ds(pl.multiple_of(th * 64 + tx * 16, 16), 16)
        send(xp_b.at[k], xp_in.at[j], xc_s.at[j], xc_r.at[j], (l, r, tx * 2 + th))
    own_k = pl.ds(pl.multiple_of(h * 64 + x * 16, 16), 16)
    total = xp_f[own_k, :]
    for j in range(7):
        arrive(xp_in.at[j], xc_s.at[j], xc_r.at[j])
        total = total + xp_in[j].astype(F32)
    rb_all[r] = total.astype(BF)

    for j, d in enumerate(Y_ORDER):
        send(rb_all.at[r], rb_all.at[r], rb_s.at[j], rb_r.at[j], (l, yat(d), q))
    xr_all[own_k, :] = total
    for j, (dx, dh) in enumerate(COL):
        send(xr_all.at[own_k], xr_all.at[own_k], xo_s.at[j], xo_r.at[j], (l, r, xat(dx) * 2 + lax.rem(h + dh, 2)))
    for j, d in enumerate(Y_ORDER):
        arrive(rb_all.at[yat(4 - d)], rb_s.at[j], rb_r.at[j])
    root_rows = jnp.concatenate([rb_all[t] for t in range(4)], axis=1)

    for d in Z_ORDER + (0,):
        child = zat(d)
        chosen = dot(root_rows, pick[child]).astype(BF)
        if d:
            j = Z_ORDER.index(d)
            sel_out[child] = chosen
            send(sel_out.at[child], sel_in.at[l], se_s.at[j], se_r.at[j], (child, r, q))
        else:
            sel_in[l] = chosen
    for j, (dx, dh) in enumerate(COL):
        k = pl.ds(pl.multiple_of(lax.rem(h + dh, 2) * 64 + xat(4 - dx) * 16, 16), 16)
        arrive(xr_all.at[k], xo_s.at[j], xo_r.at[j])
    flip[...] = xr_all[...].T
    xroot_ref[...] = flip[pl.ds(pl.multiple_of(q * 48, 16), 48), :]
    for d in Z_ARRIVAL:
        j = Z_ORDER.index((8 - d) % 8)
        arrive(sel_in.at[zat(d)], se_s.at[j], se_r.at[j])

    for j, (dy, dx) in enumerate(PLANE):
        send(sel_in, sel_all.at[r, x], pl_s.at[j], pl_r.at[j], (l, yat(dy), xat(dx) * 2 + h))
    sel_all[r, x] = sel_in[...]
    arrive(back_v.at[1 - h], w_s.at[0], w_r.at[0])
    arrive(bwd_v.at[1 - h], w_s.at[1], w_r.at[1])
    corr = jnp.zeros((64, 384), F32)
    for dy in (0, 1, 3, 2):
        sr = yat(dy)
        for dx in (0, 1, 3, 2):
            if dy or dx:
                j = PLANE.index(((4 - dy) % 4, (4 - dx) % 4))
                arrive(sel_all.at[sr, xat(dx)], pl_s.at[j], pl_r.at[j])
        left = jnp.concatenate([sel_all[sr, :, b].reshape(64, 128) for b in range(8)], axis=1)
        right = jnp.concatenate(
            [
                back_v[:, :, pl.ds(pl.multiple_of(b * 512 + sr * 128, 128), 128)].reshape(384, 128)
                for b in range(8)
            ],
            axis=1,
        )
        corr = corr + dot_last(left, right)
    reduced = (y_keep[...] - corr).astype(BF)

    for j, (dy, dx) in enumerate(PLANE + [(0, 0)]):
        cols = pl.ds(pl.multiple_of((yat(dy) * 4 + xat(dx)) * 384, 128), 384)
        value = dot(reduced, bwd_v[:, :, cols].reshape(384, 384))
        if dy or dx:
            z_out[j] = value.astype(BF)
            send(z_out.at[j], z_in.at[j], fin_s.at[j], fin_r.at[j], (l, yat(dy), xat(dx) * 2 + h))
    total = value
    flush()
    for j in range(14, -1, -1):
        arrive(z_in.at[j], fin_s.at[j], fin_r.at[j])
        total = total + z_in[j].astype(F32)

    zsum[mine, :] = total
    send(zsum.at[mine], zsum.at[mine], end_s.at[0], end_r.at[0], sib)
    arrive(zsum.at[other], end_s.at[0], end_r.at[0])
    flip[...] = zsum[...].T
    xchild_ref[...] = flip[pl.ds(pl.multiple_of(h * 192, 64), 192), :]
    flush()


def local(
    rhs_child, rhs_root, fwd_child, coupling, root_inverse, back_child, bwd_child, parent_rows
):
    vm = pltpu.VMEM
    dma = pltpu.SemaphoreType.DMA
    scratch = [
        vm((128, 768), BF), vm((4, 768, 384), BF), vm((1536, 512), BF), vm((1536, 384), BF),
        vm((2, 192, 4096), BF), vm((2, 192, 6144), BF), vm((32, 1536), F32), vm((8, 1, 4096), jnp.int32),
        vm((4, 128, 384), F32), vm((4, 128, 384), BF), vm((4, 64, 384), BF), vm((3, 64, 384), BF),
        vm((3, 64, 384), BF), vm((64, 384), F32), vm((4, 128, 384), BF),
        vm((128, 512), F32), vm((128, 512), BF), vm((3, 32, 512), BF), vm((8, 32, 512), BF),
        vm((8, 1536, 512), BF), vm((8, 1536, 128), BF), vm((128, 1536), BF),
        vm((128, 384), F32), vm((128, 384), BF), vm((7, 16, 384), BF), vm((128, 384), F32),
        vm((4, 16, 384), BF), vm((8, 16, 128), BF), vm((8, 16, 128), BF), vm((4, 4, 8, 16, 128), BF),
        vm((15, 64, 384), BF), vm((15, 64, 384), BF), vm((128, 384), F32), vm((384, 128), F32),
        dma((11,)),
    ]
    for n in (4, 3, 3, 4, 3, 7, 7, 3, 7, 7, 3, 7, 15, 15, 1, 2):
        scratch += [dma((n,)), dma((n,))]
    any_spec = pl.BlockSpec(memory_space=pl.ANY)
    vm_spec = pl.BlockSpec(memory_space=pltpu.VMEM)
    x_root, x_child = pl.pallas_call(
        kernel,
        out_shape=(jax.ShapeDtypeStruct((48, 128), F32), jax.ShapeDtypeStruct((192, 128), F32)),
        in_specs=[any_spec] * 8,
        out_specs=(vm_spec, vm_spec),
        scratch_shapes=scratch,
        compiler_params=pltpu.CompilerParams(
            collective_id=0, has_side_effects=True, vmem_limit_bytes=56 * 2**20
        ),
    )(
        rhs_child[0], rhs_root, fwd_child[0], coupling[0], root_inverse, back_child[0].T, bwd_child[0], parent_rows
    )
    return (x_root.T, x_child.T[None])


def solution(mesh):
    placed = (
        P("leaf", None, "col"),
        P(None, "col"),
        P("leaf", "col", "row"),
        P("leaf", "row", "col"),
        P("col", ("leaf", "row")),
        P("leaf", None, ("row", "col")),
        P("leaf", ("row", "col"), None),
        P("leaf", None),
    )
    return jax.shard_map(
        local,
        mesh=mesh,
        in_specs=placed,
        out_specs=(P(None, ("leaf", "row", "col")), P("leaf", None, ("row", "col"))),
        check_vma=False,
    )
```

```python
import jax
import jax.numpy as jnp
from jax import lax
from jax.experimental import pallas as pl
from jax.experimental.pallas import tpu as pltpu
from jax.sharding import PartitionSpec as P

BF = jnp.bfloat16
F32 = jnp.float32
MESH = pl.DeviceIdType.MESH
CONTRACT_LAST = (((1,), (1,)), ((), ()))

X_ORDER = (2, 1, 3)
Y_ORDER = (2, 1, 3)
Z_ORDER = (4, 3, 5, 2, 6, 1, 7)
Z_ARRIVAL = (4, 3, 5, 2, 6, 1, 7)
PLANE = sorted(
    ((dy, dx) for dy in range(4) for dx in range(4) if (dy, dx) != (0, 0)),
    key=lambda p: -(min(p[0], 4 - p[0]) + min(p[1], 4 - p[1])),
)
COL = [(dx, dh) for dx in (2, 1, 3) for dh in (1, 0)] + [(0, 1)]


def dot(a, b):
    return jnp.dot(a, b, preferred_element_type=F32)


def dot_last(a, b):
    return lax.dot_general(a, b, CONTRACT_LAST, preferred_element_type=F32)


def kernel(
    rhs_ref, root_ref, fwd_ref, coup_ref, rinv_ref, back_ref, bwd_ref, rows_ref,
    both_ref,
    rhs_v, fwd_v, coup_v, rinv_v, back_v, bwd_v, root_v, rows_v,
    part_f, part_b, core_in, x_f, x_out, x_in, y_keep,
    u_f, u_b, u_in, u_all, place, pick, p_rhs,
    xp_f, xp_b, xp_in, xr_all, rb_all, sel_out, sel_in, sel_all,
    z_out, z_in, zsum, flip,
    load_sem, core_s, core_r, xs_s, xs_r,
    us_s, us_r, za_s, za_r, pr_s, pr_r, ya_s, ya_r, xc_s, xc_r, xo_s, xo_r,
    rb_s, rb_r, se_s, se_r, pl_s, pl_r, fin_s, fin_r, end_s, end_r, w_s, w_r,
):
    l, r, q = lax.axis_index("leaf"), lax.axis_index("row"), lax.axis_index("col")
    x, h = q // 2, q % 2
    sib = (l, r, x * 2 + 1 - h)

    def xat(d):
        return lax.rem(x + d, 4)

    def yat(d):
        return lax.rem(r + d, 4)

    def zat(d):
        return lax.rem(l + d, 8)

    def load(src, dst, k):
        c = pltpu.make_async_copy(src, dst, load_sem.at[k])
        c.start()
        return c

    pending = []

    def send(src, dst, ss, rs, device):
        c = pltpu.make_async_remote_copy(
            src_ref=src, dst_ref=dst, send_sem=ss, recv_sem=rs, device_id=device, device_id_type=MESH
        )
        c.start()
        pending.append(c)

    def arrive(dst, ss, rs):
        pltpu.make_async_remote_copy(
            src_ref=dst, dst_ref=dst, send_sem=ss, recv_sem=rs, device_id=sib, device_id_type=MESH
        ).wait_recv()

    def flush():
        while pending:
            pending.pop(0).wait_send()

    partners = [(l, r, xat(dx) * 2 + lax.rem(h + dh, 2)) for dx, dh in COL]
    partners += [(l, yat(dy), xat(dx) * 2 + h) for dy, dx in PLANE if dy]
    partners += [(l, yat(d), x * 2 + 1 - h) for d in Y_ORDER]
    partners += [(zat(d), r, q) for d in Z_ORDER]
    bar = pltpu.get_barrier_semaphore()
    for p in partners:
        pl.semaphore_signal(bar, inc=1, device_id=p, device_id_type=MESH)

    l_rhs = load(rhs_ref, rhs_v, 0)
    l_fwd = [load(fwd_ref.at[:, pl.ds(j * 384, 384)], fwd_v.at[j], 1 + j) for j in range(4)]
    l_coup = load(coup_ref, coup_v.at[h], 6)
    l_rows = load(rows_ref, rows_v.at[l], 5)
    l_root = [
        load(root_ref.at[pl.ds(pl.multiple_of(g * 64 + r * 16, 16), 16)], root_v.at[pl.ds(g * 16, 16)], 11 + g)
        for g in range(2)
    ]
    l_rinv = load(rinv_ref, rinv_v, 8)
    l_back = load(back_ref, back_v.at[h], 9)
    l_bwd = load(bwd_ref, bwd_v.at[h], 10)

    mine = pl.ds(pl.multiple_of(h * 64, 64), 64)
    other = pl.ds(pl.multiple_of((1 - h) * 64, 64), 64)
    l_rhs.wait()
    for j in range(4):
        l_fwd[j].wait()
        value = dot(rhs_v[...], fwd_v[j])
        part_f[j] = value
        part_b[j] = value.astype(BF)
        if j == 0:
            pl.semaphore_wait(bar, len(partners))
        send(part_b.at[j, other], core_in.at[j], core_s.at[j], core_r.at[j], sib)
    l_coup.wait()
    send(coup_v.at[h], coup_v.at[h], w_s.at[2], w_r.at[2], sib)
    for j in range(4):
        arrive(core_in.at[j], core_s.at[j], core_r.at[j])
        both = part_f[j, mine, :] + core_in[j].astype(F32)
        x_f[j] = both
        x_out[j] = both.astype(BF)
        for i, d in enumerate(X_ORDER):
            send(x_out.at[j], x_in.at[i, j], xs_s.at[i, j], xs_r.at[i, j], (l, r, xat(d) * 2 + h))

    l_rows.wait()
    for j, d in enumerate(Z_ORDER):
        send(rows_ref, rows_v.at[l], pr_s.at[j], pr_r.at[j], (zat(d), r, q))

    def build_place(leaf):
        row = rows_v[leaf, :, pl.ds(pl.multiple_of(q * 512, 512), 512)] - q * 1536

        @pl.loop(0, 12)
        def _(t):
            at = lax.broadcasted_iota(jnp.int32, (128, 512), 0) + t * 128
            place[leaf, pl.ds(pl.multiple_of(t * 128, 128), 128), :] = (at == row).astype(F32).astype(BF)

    def build_pick(leaf):
        row = rows_v[leaf, :, pl.ds(pl.multiple_of(l * 512 + r * 128, 128), 128)] - l * 1536

        @pl.loop(0, 12)
        def _(t):
            at = lax.broadcasted_iota(jnp.int32, (128, 128), 0) + t * 128
            pick[leaf, pl.ds(pl.multiple_of(t * 128, 128), 128), :] = (at == row).astype(F32).astype(BF)

    def rows_arrive(d):
        j = Z_ORDER.index((8 - d) % 8)
        arrive(rows_v.at[zat(d)], pr_s.at[j], pr_r.at[j])

    build_place(l)
    build_pick(l)
    for d in Z_ARRIVAL:
        rows_arrive(d)
        build_place(zat(d))
        build_pick(zat(d))

    arrive(coup_v.at[1 - h], w_s.at[2], w_r.at[2])
    update = [jnp.zeros((64, 512), F32) for _ in range(2)]
    for j in range(4):
        total = x_f[j]
        for i in range(3):
            arrive(x_in.at[i, j], xs_s.at[i, j], xs_r.at[i, j])
            total = total + x_in[i, j].astype(F32)
        x_f[j] = total
        left = total.astype(BF)
        for g in range(2):
            update[g] = update[g] + dot(left, coup_v[g, pl.ds(j * 384, 384), :])
    y_keep[...] = x_f[x]

    for g in range(2):
        u_f[g] = update[g]
        u_b[g] = update[g].astype(BF)
    for g in (0, 1):
        core = lax.rem(h + g, 2)
        for i, d in enumerate(Y_ORDER + ((0,) if g else ())):
            k = pl.ds(pl.multiple_of(yat(d) * 16, 16), 16)
            send(
                u_b.at[core, k], u_in.at[g, i], us_s.at[g, i], us_r.at[g, i], (l, yat(d), x * 2 + core)
            )
    l_back.wait()
    l_bwd.wait()
    send(back_v.at[h], back_v.at[h], w_s.at[0], w_r.at[0], sib)
    send(bwd_v.at[h], bwd_v.at[h], w_s.at[1], w_r.at[1], sib)
    total = u_f[h, pl.ds(pl.multiple_of(r * 16, 16), 16), :]
    for i in range(3):
        arrive(u_in.at[0, i], us_s.at[0, i], us_r.at[0, i])
        total = total + u_in[0, i].astype(F32)
    u_all[l, pl.ds(pl.multiple_of(h * 16, 16), 16), :] = total.astype(BF)
    total = jnp.zeros((16, 512), F32)
    for i in range(4):
        arrive(u_in.at[1, i], us_s.at[1, i], us_r.at[1, i])
        total = total + u_in[1, i].astype(F32)
    u_all[l, pl.ds(pl.multiple_of((1 - h) * 16, 16), 16), :] = total.astype(BF)

    for j, d in enumerate(Z_ORDER):
        send(u_all.at[l], u_all.at[l], za_s.at[j], za_r.at[j], (zat(d), r, q))
    for c in l_root:
        c.wait()
    placed = root_v[...] - dot_last(u_all[l], place[l])
    for d in Z_ARRIVAL[:6]:
        j = Z_ORDER.index((8 - d) % 8)
        leaf = zat(d)
        arrive(u_all.at[leaf], za_s.at[j], za_r.at[j])
        placed = placed - dot_last(u_all[leaf], place[leaf])
    d = Z_ARRIVAL[6]
    leaf = zat(d)
    arrive(u_all.at[leaf], za_s.at[Z_ORDER.index((8 - d) % 8)], za_r.at[Z_ORDER.index((8 - d) % 8)])

    for t in range(2):
        cols = slice(t * 768, t * 768 + 768)
        p_rhs[t, r] = (placed[:, cols] - dot_last(u_all[leaf], place[leaf, cols, :])).astype(BF)
        for i, d in enumerate(Y_ORDER):
            send(p_rhs.at[t, r], p_rhs.at[t, r], ya_s.at[t, i], ya_r.at[t, i], (l, yat(d), q))
    l_rinv.wait()
    value = jnp.zeros((128, 384), F32)
    for t in range(2):
        for i, d in enumerate(Y_ORDER):
            arrive(p_rhs.at[t, yat(4 - d)], ya_s.at[t, i], ya_r.at[t, i])
        value = value + dot(p_rhs[t].reshape(128, 768), rinv_v[pl.ds(t * 768, 768), :])

    xp_f[...] = value
    xp_b[...] = value.astype(BF)
    for j, (dx, dh) in enumerate(COL):
        tx, th = xat(dx), lax.rem(h + dh, 2)
        k = pl.ds(pl.multiple_of(tx * 32 + th * 16, 16), 16)
        send(xp_b.at[k], xp_in.at[j], xc_s.at[j], xc_r.at[j], (l, r, tx * 2 + th))
    own_k = pl.ds(pl.multiple_of(h * 64 + x * 16, 16), 16)
    total = xp_f[pl.ds(pl.multiple_of(x * 32 + h * 16, 16), 16), :]
    for j in range(7):
        arrive(xp_in.at[j], xc_s.at[j], xc_r.at[j])
        total = total + xp_in[j].astype(F32)
    rb_all[r] = total.astype(BF)

    for j, d in enumerate(Y_ORDER):
        send(rb_all.at[r], rb_all.at[r], rb_s.at[j], rb_r.at[j], (l, yat(d), q))
    xr_all[own_k, :] = total
    for j, (dx, dh) in enumerate(COL):
        send(xr_all.at[own_k], xr_all.at[own_k], xo_s.at[j], xo_r.at[j], (l, r, xat(dx) * 2 + lax.rem(h + dh, 2)))
    for j, d in enumerate(Y_ORDER):
        arrive(rb_all.at[yat(4 - d)], rb_s.at[j], rb_r.at[j])
    root_rows = jnp.concatenate([rb_all[t] for t in range(4)], axis=1)

    for d in Z_ORDER + (0,):
        child = zat(d)
        chosen = dot(root_rows, pick[child]).astype(BF)
        if d:
            j = Z_ORDER.index(d)
            sel_out[child] = chosen
            send(sel_out.at[child], sel_in.at[l], se_s.at[j], se_r.at[j], (child, r, q))
        else:
            sel_in[l] = chosen
    for j, (dx, dh) in enumerate(COL):
        k = pl.ds(pl.multiple_of(lax.rem(h + dh, 2) * 64 + xat(4 - dx) * 16, 16), 16)
        arrive(xr_all.at[k], xo_s.at[j], xo_r.at[j])
    flip[...] = xr_all[...].T
    both_ref[0:48, :] = flip[pl.ds(pl.multiple_of(q * 48, 16), 48), :]
    for d in Z_ARRIVAL:
        j = Z_ORDER.index((8 - d) % 8)
        arrive(sel_in.at[zat(d)], se_s.at[j], se_r.at[j])

    for j, (dy, dx) in enumerate(PLANE):
        send(sel_in, sel_all.at[r, x], pl_s.at[j], pl_r.at[j], (l, yat(dy), xat(dx) * 2 + h))
    sel_all[r, x] = sel_in[...]
    arrive(back_v.at[1 - h], w_s.at[0], w_r.at[0])
    arrive(bwd_v.at[1 - h], w_s.at[1], w_r.at[1])
    corr = jnp.zeros((64, 384), F32)
    for dy in (0, 1, 3, 2):
        sr = yat(dy)
        for dx in (0, 1, 3, 2):
            if dy or dx:
                j = PLANE.index(((4 - dy) % 4, (4 - dx) % 4))
                arrive(sel_all.at[sr, xat(dx)], pl_s.at[j], pl_r.at[j])
        left = jnp.concatenate([sel_all[sr, :, b].reshape(64, 128) for b in range(8)], axis=1)
        right = jnp.concatenate(
            [
                back_v[:, :, pl.ds(pl.multiple_of(b * 512 + sr * 128, 128), 128)].reshape(384, 128)
                for b in range(8)
            ],
            axis=1,
        )
        corr = corr + dot_last(left, right)
    reduced = (y_keep[...] - corr).astype(BF)

    for j, (dy, dx) in enumerate(PLANE + [(0, 0)]):
        cols = pl.ds(pl.multiple_of((yat(dy) * 4 + xat(dx)) * 384, 128), 384)
        value = dot(reduced, bwd_v[:, :, cols].reshape(384, 384))
        if dy or dx:
            z_out[j] = value.astype(BF)
            send(z_out.at[j], z_in.at[j], fin_s.at[j], fin_r.at[j], (l, yat(dy), xat(dx) * 2 + h))
    total = value
    flush()
    for j in range(14, -1, -1):
        arrive(z_in.at[j], fin_s.at[j], fin_r.at[j])
        total = total + z_in[j].astype(F32)

    zsum[mine, :] = total
    send(zsum.at[mine], zsum.at[mine], end_s.at[0], end_r.at[0], sib)
    arrive(zsum.at[other], end_s.at[0], end_r.at[0])
    flip[...] = zsum[...].T
    both_ref[48:240, :] = flip[pl.ds(pl.multiple_of(h * 192, 64), 192), :]
    flush()


def split(both_ref, xroot_ref, xchild_ref):
    xroot_ref[...] = both_ref[0:48, :]
    xchild_ref[...] = both_ref[48:240, :]


def local(
    rhs_child, rhs_root, fwd_child, coupling, root_inverse, back_child, bwd_child, parent_rows
):
    vm = pltpu.VMEM
    dma = pltpu.SemaphoreType.DMA
    scratch = [
        vm((128, 768), BF), vm((4, 768, 384), BF), vm((2, 1536, 512), BF), vm((1536, 384), BF),
        vm((2, 192, 4096), BF), vm((2, 192, 6144), BF), vm((32, 1536), F32), vm((8, 1, 4096), jnp.int32),
        vm((4, 128, 384), F32), vm((4, 128, 384), BF), vm((4, 64, 384), BF), vm((4, 64, 384), F32),
        vm((4, 64, 384), BF), vm((3, 4, 64, 384), BF), vm((64, 384), F32),
        vm((2, 64, 512), F32), vm((2, 64, 512), BF), vm((2, 4, 16, 512), BF), vm((8, 32, 512), BF),
        vm((8, 1536, 512), BF), vm((8, 1536, 128), BF), vm((2, 4, 32, 768), BF),
        vm((128, 384), F32), vm((128, 384), BF), vm((7, 16, 384), BF), vm((128, 384), F32),
        vm((4, 16, 384), BF), vm((8, 16, 128), BF), vm((8, 16, 128), BF), vm((4, 4, 8, 16, 128), BF),
        vm((15, 64, 384), BF), vm((15, 64, 384), BF), vm((128, 384), F32), vm((384, 128), F32),
        dma((13,)),
    ]
    for n in (4, (3, 4), (2, 4), 7, 7, (2, 3), 7, 7, 3, 7, 15, 15, 1, 3):
        n = n if isinstance(n, tuple) else (n,)
        scratch += [dma(n), dma(n)]
    any_spec = pl.BlockSpec(memory_space=pl.ANY)
    vm_spec = pl.BlockSpec(memory_space=pltpu.VMEM)
    both = pl.pallas_call(
        kernel,
        out_shape=jax.ShapeDtypeStruct((240, 128), F32),
        in_specs=[any_spec] * 8,
        out_specs=vm_spec,
        scratch_shapes=scratch,
        compiler_params=pltpu.CompilerParams(
            collective_id=0, has_side_effects=True, vmem_limit_bytes=56 * 2**20
        ),
    )(
        rhs_child[0], rhs_root, fwd_child[0], coupling[0], root_inverse, back_child[0].T, bwd_child[0], parent_rows
    )
    x_root, x_child = pl.pallas_call(
        split,
        out_shape=(jax.ShapeDtypeStruct((48, 128), F32), jax.ShapeDtypeStruct((192, 128), F32)),
        in_specs=[vm_spec],
        out_specs=(vm_spec, vm_spec),
    )(both)
    return (x_root.T, x_child.T[None])


def solution(mesh):
    placed = (
        P("leaf", None, "col"),
        P(None, "col"),
        P("leaf", "col", "row"),
        P("leaf", "row", "col"),
        P("col", ("leaf", "row")),
        P("leaf", None, ("row", "col")),
        P("leaf", ("row", "col"), None),
        P("leaf", None),
    )
    return jax.shard_map(
        local,
        mesh=mesh,
        in_specs=placed,
        out_specs=(P(None, ("leaf", "row", "col")), P("leaf", None, ("row", "col"))),
        check_vma=False,
    )
```

```python
import jax
import jax.numpy as jnp
from jax import lax
from jax.experimental import pallas as pl
from jax.experimental.pallas import tpu as pltpu
from jax.sharding import PartitionSpec as P

BF = jnp.bfloat16
F32 = jnp.float32
MESH = pl.DeviceIdType.MESH
CONTRACT_LAST = (((1,), (1,)), ((), ()))

X_ORDER = (2, 1, 3)
Y_ORDER = (2, 1, 3)
Z_ORDER = (4, 3, 5, 2, 6, 1, 7)
Z_ARRIVAL = (4, 3, 5, 2, 6, 1, 7)
PLANE = sorted(
    ((dy, dx) for dy in range(4) for dx in range(4) if (dy, dx) != (0, 0)),
    key=lambda p: -(min(p[0], 4 - p[0]) + min(p[1], 4 - p[1])),
)
OWNERS = (
    (2, 2), (2, 1), (1, 2), (2, 3), (3, 2), (2, 0), (0, 2),
    (1, 1), (1, 3), (3, 1), (1, 0), (0, 1), (3, 3), (3, 0), (0, 3), (0, 0),
)
COL = [(dx, dh) for dx in (2, 1, 3) for dh in (1, 0)] + [(0, 1)]


def dot(a, b):
    return jnp.dot(a, b, preferred_element_type=F32)


def dot_last(a, b):
    return lax.dot_general(a, b, CONTRACT_LAST, preferred_element_type=F32)


def kernel(
    rhs_ref, root_ref, fwd_ref, coup_ref, rinv_ref, back_ref, bwd_ref, rows_ref,
    both_ref,
    rhs_v, fwd_v, coup_v, rinv_v, back_v, bwd_v, root_v, rows_v,
    part_f, part_b, core_in, x_f, x_out, x_in, y_keep,
    u_f, u_b, u_in, u_all, place, pick, p_rhs,
    xp_f, xp_b, xp_in, xr_all, rb_all, sel_out, sel_in, sel_all,
    z_out, a_f, b_f, a_in, b_in, a_out, b_out, fa_in, fb_in, own_f, own_in, flip, flip2,
    load_sem, core_s, core_r, xs_s, xs_r,
    us_s, us_r, za_s, za_r, pr_s, pr_r, ya_s, ya_r, xc_s, xc_r, xo_s, xo_r,
    rb_s, rb_r, se_s, se_r, pl_s, pl_r, a_s, a_r, b_s, b_r, fa_s, fa_r, fb_s, fb_r, end_s, end_r, w_s, w_r,
):
    l, r, q = lax.axis_index("leaf"), lax.axis_index("row"), lax.axis_index("col")
    x, h = q // 2, q % 2
    sib = (l, r, x * 2 + 1 - h)

    def xat(d):
        return lax.rem(x + d, 4)

    def yat(d):
        return lax.rem(r + d, 4)

    def zat(d):
        return lax.rem(l + d, 8)

    def load(src, dst, k):
        c = pltpu.make_async_copy(src, dst, load_sem.at[k])
        c.start()
        return c

    pending = []

    def send(src, dst, ss, rs, device):
        c = pltpu.make_async_remote_copy(
            src_ref=src, dst_ref=dst, send_sem=ss, recv_sem=rs, device_id=device, device_id_type=MESH
        )
        c.start()
        pending.append(c)

    def arrive(dst, ss, rs):
        pltpu.make_async_remote_copy(
            src_ref=dst, dst_ref=dst, send_sem=ss, recv_sem=rs, device_id=sib, device_id_type=MESH
        ).wait_recv()

    def flush():
        while pending:
            pending.pop(0).wait_send()

    l_rhs = load(rhs_ref, rhs_v, 0)
    l_fwd = [load(fwd_ref.at[:, pl.ds(j * 384, 384)], fwd_v.at[j], 1 + j) for j in range(4)]
    partners = [(l, r, xat(dx) * 2 + lax.rem(h + dh, 2)) for dx, dh in COL]
    partners += [(l, yat(dy), xat(dx) * 2 + h) for dy, dx in PLANE if dy]
    partners += [(l, yat(d), x * 2 + 1 - h) for d in Y_ORDER]
    partners += [(zat(d), r, q) for d in Z_ORDER]
    bar = pltpu.get_barrier_semaphore()
    for p in partners:
        pl.semaphore_signal(bar, inc=1, device_id=p, device_id_type=MESH)

    l_coup = load(coup_ref, coup_v.at[h], 6)
    l_rows = load(rows_ref, rows_v.at[l], 5)

    mine = pl.ds(pl.multiple_of(h * 64, 64), 64)
    other = pl.ds(pl.multiple_of((1 - h) * 64, 64), 64)
    l_rhs.wait()
    for j in range(4):
        l_fwd[j].wait()
        value = dot(rhs_v[...], fwd_v[j])
        part_f[j] = value
        part_b[j] = value.astype(BF)
        if j == 0:
            pl.semaphore_wait(bar, len(partners))
        send(part_b.at[j, other], core_in.at[j], core_s.at[j], core_r.at[j], sib)
    l_root = [
        load(root_ref.at[pl.ds(pl.multiple_of(g * 64 + r * 16, 16), 16)], root_v.at[pl.ds(g * 16, 16)], 11 + g)
        for g in range(2)
    ]
    l_rinv = load(rinv_ref, rinv_v, 8)
    l_back = load(back_ref, back_v.at[h], 9)
    l_bwd = load(bwd_ref, bwd_v.at[h], 10)
    l_coup.wait()
    send(coup_v.at[h], coup_v.at[h], w_s.at[2], w_r.at[2], sib)
    for j in range(4):
        arrive(core_in.at[j], core_s.at[j], core_r.at[j])
        both = part_f[j, mine, :] + core_in[j].astype(F32)
        x_f[j] = both
        x_out[j] = both.astype(BF)
        for i, d in enumerate(X_ORDER):
            send(x_out.at[j], x_in.at[i, j], xs_s.at[i, j], xs_r.at[i, j], (l, r, xat(d) * 2 + h))

    l_rows.wait()
    for j, d in enumerate(Z_ORDER):
        send(rows_ref, rows_v.at[l], pr_s.at[j], pr_r.at[j], (zat(d), r, q))

    def build_place(leaf):
        row = rows_v[leaf, :, pl.ds(pl.multiple_of(q * 512, 512), 512)] - q * 1536

        @pl.loop(0, 12)
        def _(t):
            at = lax.broadcasted_iota(jnp.int32, (128, 512), 0) + t * 128
            place[leaf, pl.ds(pl.multiple_of(t * 128, 128), 128), :] = (at == row).astype(F32).astype(BF)

    def build_pick(leaf):
        row = rows_v[leaf, :, pl.ds(pl.multiple_of(l * 512 + r * 128, 128), 128)] - l * 1536

        @pl.loop(0, 12)
        def _(t):
            at = lax.broadcasted_iota(jnp.int32, (128, 128), 0) + t * 128
            pick[leaf, pl.ds(pl.multiple_of(t * 128, 128), 128), :] = (at == row).astype(F32).astype(BF)

    def rows_arrive(d):
        j = Z_ORDER.index((8 - d) % 8)
        arrive(rows_v.at[zat(d)], pr_s.at[j], pr_r.at[j])

    build_place(l)
    for d in (1, 7, 2, 6):
        rows_arrive(d)
        build_place(zat(d))

    arrive(coup_v.at[1 - h], w_s.at[2], w_r.at[2])
    update = [jnp.zeros((64, 512), F32) for _ in range(2)]
    for j in range(4):
        total = x_f[j]
        for i in range(3):
            arrive(x_in.at[i, j], xs_s.at[i, j], xs_r.at[i, j])
            total = total + x_in[i, j].astype(F32)
        x_f[j] = total
        left = total.astype(BF)
        for g in range(2):
            update[g] = update[g] + dot(left, coup_v[g, pl.ds(j * 384, 384), :])
    y_keep[...] = x_f[x]

    for g in range(2):
        u_f[g] = update[g]
        u_b[g] = update[g].astype(BF)
    for g in (0, 1):
        core = lax.rem(h + g, 2)
        for i, d in enumerate(Y_ORDER + ((0,) if g else ())):
            k = pl.ds(pl.multiple_of(yat(d) * 16, 16), 16)
            send(
                u_b.at[core, k], u_in.at[g, i], us_s.at[g, i], us_r.at[g, i], (l, yat(d), x * 2 + core)
            )
    l_back.wait()
    l_bwd.wait()
    send(back_v.at[h], back_v.at[h], w_s.at[0], w_r.at[0], sib)
    send(bwd_v.at[h], bwd_v.at[h], w_s.at[1], w_r.at[1], sib)
    for d in (3, 5, 4):
        rows_arrive(d)
        build_place(zat(d))
    total = u_f[h, pl.ds(pl.multiple_of(r * 16, 16), 16), :]
    for i in range(3):
        arrive(u_in.at[0, i], us_s.at[0, i], us_r.at[0, i])
        total = total + u_in[0, i].astype(F32)
    u_all[l, pl.ds(pl.multiple_of(h * 16, 16), 16), :] = total.astype(BF)
    total = jnp.zeros((16, 512), F32)
    for i in range(4):
        arrive(u_in.at[1, i], us_s.at[1, i], us_r.at[1, i])
        total = total + u_in[1, i].astype(F32)
    u_all[l, pl.ds(pl.multiple_of((1 - h) * 16, 16), 16), :] = total.astype(BF)

    for j, d in enumerate(Z_ORDER):
        send(u_all.at[l], u_all.at[l], za_s.at[j], za_r.at[j], (zat(d), r, q))
    for c in l_root:
        c.wait()
    placed = root_v[...] - dot_last(u_all[l], place[l])
    for d in Z_ARRIVAL[:6]:
        j = Z_ORDER.index((8 - d) % 8)
        leaf = zat(d)
        arrive(u_all.at[leaf], za_s.at[j], za_r.at[j])
        placed = placed - dot_last(u_all[leaf], place[leaf])
    d = Z_ARRIVAL[6]
    leaf = zat(d)
    arrive(u_all.at[leaf], za_s.at[Z_ORDER.index((8 - d) % 8)], za_r.at[Z_ORDER.index((8 - d) % 8)])

    for t in range(2):
        cols = slice(t * 768, t * 768 + 768)
        p_rhs[t, r] = (placed[:, cols] - dot_last(u_all[leaf], place[leaf, cols, :])).astype(BF)
        for i, d in enumerate(Y_ORDER):
            send(p_rhs.at[t, r], p_rhs.at[t, r], ya_s.at[t, i], ya_r.at[t, i], (l, yat(d), q))
    for d in range(8):
        build_pick(zat(d))
    l_rinv.wait()
    value = jnp.zeros((128, 384), F32)
    for t in range(2):
        for i, d in enumerate(Y_ORDER):
            arrive(p_rhs.at[t, yat(4 - d)], ya_s.at[t, i], ya_r.at[t, i])
        value = value + dot(p_rhs[t].reshape(128, 768), rinv_v[pl.ds(t * 768, 768), :])

    xp_f[...] = value
    xp_b[...] = value.astype(BF)
    for j, (dx, dh) in enumerate(COL):
        tx, th = xat(dx), lax.rem(h + dh, 2)
        k = pl.ds(pl.multiple_of(tx * 32 + th * 16, 16), 16)
        send(xp_b.at[k], xp_in.at[j], xc_s.at[j], xc_r.at[j], (l, r, tx * 2 + th))
    own_k = pl.ds(pl.multiple_of(h * 64 + x * 16, 16), 16)
    total = xp_f[pl.ds(pl.multiple_of(x * 32 + h * 16, 16), 16), :]
    for j in range(7):
        arrive(xp_in.at[j], xc_s.at[j], xc_r.at[j])
        total = total + xp_in[j].astype(F32)
    rb_all[r] = total.astype(BF)

    for j, d in enumerate(Y_ORDER):
        send(rb_all.at[r], rb_all.at[r], rb_s.at[j], rb_r.at[j], (l, yat(d), q))
    xr_all[own_k, :] = total
    for j, (dx, dh) in enumerate(COL):
        send(xr_all.at[own_k], xr_all.at[own_k], xo_s.at[j], xo_r.at[j], (l, r, xat(dx) * 2 + lax.rem(h + dh, 2)))
    for j, d in enumerate(Y_ORDER):
        arrive(rb_all.at[yat(4 - d)], rb_s.at[j], rb_r.at[j])
    root_rows = jnp.concatenate([rb_all[t] for t in range(4)], axis=1)

    for d in Z_ORDER + (0,):
        child = zat(d)
        chosen = dot(root_rows, pick[child]).astype(BF)
        if d:
            j = Z_ORDER.index(d)
            sel_out[child] = chosen
            send(sel_out.at[child], sel_in.at[l], se_s.at[j], se_r.at[j], (child, r, q))
        else:
            sel_in[l] = chosen
    for j, (dx, dh) in enumerate(COL):
        k = pl.ds(pl.multiple_of(lax.rem(h + dh, 2) * 64 + xat(4 - dx) * 16, 16), 16)
        arrive(xr_all.at[k], xo_s.at[j], xo_r.at[j])
    flip[...] = xr_all[...].T
    both_ref[0:48, :] = flip[pl.ds(pl.multiple_of(q * 48, 16), 48), :]
    for d in Z_ARRIVAL:
        j = Z_ORDER.index((8 - d) % 8)
        arrive(sel_in.at[zat(d)], se_s.at[j], se_r.at[j])

    for j, (dy, dx) in enumerate(PLANE):
        send(sel_in, sel_all.at[r, x], pl_s.at[j], pl_r.at[j], (l, yat(dy), xat(dx) * 2 + h))
    sel_all[r, x] = sel_in[...]
    arrive(back_v.at[1 - h], w_s.at[0], w_r.at[0])
    arrive(bwd_v.at[1 - h], w_s.at[1], w_r.at[1])
    corr = jnp.zeros((64, 384), F32)
    for dy in (0, 1, 3, 2):
        sr = yat(dy)
        for dx in (0, 1, 3, 2):
            if dy or dx:
                j = PLANE.index(((4 - dy) % 4, (4 - dx) % 4))
                arrive(sel_all.at[sr, xat(dx)], pl_s.at[j], pl_r.at[j])
        left = jnp.concatenate([sel_all[sr, :, b].reshape(64, 128) for b in range(8)], axis=1)
        right = jnp.concatenate(
            [
                back_v[:, :, pl.ds(pl.multiple_of(b * 512 + sr * 128, 128), 128)].reshape(384, 128)
                for b in range(8)
            ],
            axis=1,
        )
        corr = corr + dot_last(left, right)
    reduced = (y_keep[...] - corr).astype(BF)

    for j, (dy, dx) in enumerate(OWNERS):
        cols = pl.ds(pl.multiple_of((yat(dy) * 4 + xat(dx)) * 384, 128), 384)
        value = dot(reduced, bwd_v[:, :, cols].reshape(384, 384))
        z_out[j] = value.astype(BF)
        if dx:
            send(z_out.at[j, 0:32], a_in.at[dy, dx - 1], a_s.at[dy, dx - 1], a_r.at[dy, dx - 1], (l, r, xat(dx) * 2 + h))
        else:
            a_f[dy] = value[0:32]
        if dy:
            send(z_out.at[j, 32:64], b_in.at[dx, dy - 1], b_s.at[dx, dy - 1], b_r.at[dx, dy - 1], (l, yat(dy), x * 2 + h))
        else:
            b_f[dx] = value[32:64]
    for c in pending[:-24]:
        c.wait_send()
    del pending[:-24]
    for d in (2, 1, 3, 0):
        for first, came, s_sem, r_sem, on, fin, fin_s, fin_r, at in (
            (a_f, a_in, a_s, a_r, a_out, fa_in, fa_s, fa_r, 0), (b_f, b_in, b_s, b_r, b_out, fb_in, fb_s, fb_r, 32)
        ):
            total = first[d]
            for i in range(3):
                arrive(came.at[d, i], s_sem.at[d, i], r_sem.at[d, i])
                total = total + came[d, i].astype(F32)
            if d:
                on[d - 1] = total.astype(BF)
                for g in range(2):
                    to = (l, r, xat(d) * 2 + g) if at else (l, yat(d), x * 2 + g)
                    send(on.at[d - 1, :, g * 128 : g * 128 + 256], fin.at[h, d - 1], fin_s.at[g, d - 1], fin_r.at[h, d - 1], to)
            else:
                own_f[at : at + 32, :] = total

    send(
        own_f.at[:, pl.ds(pl.multiple_of((1 - h) * 128, 128), 256)], own_in.at[h], end_s.at[0], end_r.at[0], sib
    )
    own_in[h] = own_f[:, pl.ds(pl.multiple_of(h * 128, 128), 256)]
    flush()
    arrive(own_in.at[1 - h], end_s.at[0], end_r.at[0])
    for d in (2, 1, 3):
        for fin, fin_s, fin_r, at in ((fa_in, fa_s, fa_r, 0), (fb_in, fb_s, fb_r, 32)):
            for c in range(2):
                arrive(fin.at[c, d - 1], fin_s.at[c, d - 1], fin_r.at[c, d - 1])
                own_in[c, at : at + 32] = own_in[c, at : at + 32] + fin[c, d - 1].astype(F32)
    flip2[...] = own_in[...].reshape(128, 256).T
    both_ref[48:240, :] = flip2[pl.ds(pl.multiple_of(h * 64, 64), 192), :]


def split(both_ref, xroot_ref, xchild_ref):
    xroot_ref[...] = both_ref[0:48, :]
    xchild_ref[...] = both_ref[48:240, :]


def local(
    rhs_child, rhs_root, fwd_child, coupling, root_inverse, back_child, bwd_child, parent_rows
):
    vm = pltpu.VMEM
    dma = pltpu.SemaphoreType.DMA
    scratch = [
        vm((128, 768), BF), vm((4, 768, 384), BF), vm((2, 1536, 512), BF), vm((1536, 384), BF),
        vm((2, 192, 4096), BF), vm((2, 192, 6144), BF), vm((32, 1536), F32), vm((8, 1, 4096), jnp.int32),
        vm((4, 128, 384), F32), vm((4, 128, 384), BF), vm((4, 64, 384), BF), vm((4, 64, 384), F32),
        vm((4, 64, 384), BF), vm((3, 4, 64, 384), BF), vm((64, 384), F32),
        vm((2, 64, 512), F32), vm((2, 64, 512), BF), vm((2, 4, 16, 512), BF), vm((8, 32, 512), BF),
        vm((8, 1536, 512), BF), vm((8, 1536, 128), BF), vm((2, 4, 32, 768), BF),
        vm((128, 384), F32), vm((128, 384), BF), vm((7, 16, 384), BF), vm((128, 384), F32),
        vm((4, 16, 384), BF), vm((8, 16, 128), BF), vm((8, 16, 128), BF), vm((4, 4, 8, 16, 128), BF),
        vm((16, 64, 384), BF), vm((4, 32, 384), F32), vm((4, 32, 384), F32),
        vm((4, 3, 32, 384), BF), vm((4, 3, 32, 384), BF), vm((3, 32, 384), BF), vm((3, 32, 384), BF),
        vm((2, 3, 32, 256), BF), vm((2, 3, 32, 256), BF), vm((64, 384), F32), vm((2, 64, 256), F32),
        vm((384, 128), F32), vm((256, 128), F32),
        dma((13,)),
    ]
    for n in (4, (3, 4), (2, 4), 7, 7, (2, 3), 7, 7, 3, 7, 15, (4, 3), (4, 3), (2, 3), (2, 3), 1, 3):
        n = n if isinstance(n, tuple) else (n,)
        scratch += [dma(n), dma(n)]
    any_spec = pl.BlockSpec(memory_space=pl.ANY)
    vm_spec = pl.BlockSpec(memory_space=pltpu.VMEM)
    both = pl.pallas_call(
        kernel,
        out_shape=jax.ShapeDtypeStruct((240, 128), F32),
        in_specs=[any_spec] * 8,
        out_specs=vm_spec,
        scratch_shapes=scratch,
        compiler_params=pltpu.CompilerParams(
            collective_id=0, has_side_effects=True, vmem_limit_bytes=56 * 2**20
        ),
    )(
        rhs_child[0], rhs_root, fwd_child[0], coupling[0], root_inverse, back_child[0].T, bwd_child[0], parent_rows
    )
    x_root, x_child = pl.pallas_call(
        split,
        out_shape=(jax.ShapeDtypeStruct((48, 128), F32), jax.ShapeDtypeStruct((192, 128), F32)),
        in_specs=[vm_spec],
        out_specs=(vm_spec, vm_spec),
    )(both)
    return (x_root.T, x_child.T[None])


def solution(mesh):
    placed = (
        P("leaf", None, "col"),
        P(None, "col"),
        P("leaf", "col", "row"),
        P("leaf", "row", "col"),
        P("col", ("leaf", "row")),
        P("leaf", None, ("row", "col")),
        P("leaf", ("row", "col"), None),
        P("leaf", None),
    )
    return jax.shard_map(
        local,
        mesh=mesh,
        in_specs=placed,
        out_specs=(P(None, ("leaf", "row", "col")), P("leaf", None, ("row", "col"))),
        check_vma=False,
    )
```

```python
import jax
import jax.numpy as jnp
from jax import lax
from jax.experimental import pallas as pl
from jax.experimental.pallas import tpu as pltpu
from jax.sharding import PartitionSpec as P

BF = jnp.bfloat16
F32 = jnp.float32
MESH = pl.DeviceIdType.MESH
CONTRACT_LAST = (((1,), (1,)), ((), ()))

X_ORDER = (2, 1, 3)
NEAR = (0, 1, 7, 2, 6, 3, 5, 4)
GROUPS = ((0, 5), (5, 8))
X_BLOCKS = X_ORDER + (0,)
Y_ORDER = (2, 1, 3)
Z_ORDER = (4, 3, 5, 2, 6, 1, 7)
Z_ARRIVAL = (4, 3, 5, 2, 6, 1, 7)
PLANE = sorted(
    ((dy, dx) for dy in range(4) for dx in range(4) if (dy, dx) != (0, 0)),
    key=lambda p: -(min(p[0], 4 - p[0]) + min(p[1], 4 - p[1])),
)
OWNERS = (
    (2, 2), (2, 1), (1, 2), (2, 3), (3, 2), (2, 0), (0, 2),
    (1, 1), (1, 3), (3, 1), (1, 0), (0, 1), (3, 3), (3, 0), (0, 3), (0, 0),
)
COL = [(dx, dh) for dx in (2, 1, 3) for dh in (1, 0)] + [(0, 1)]


def dot(a, b):
    return jnp.dot(a, b, preferred_element_type=F32)


def dot_last(a, b):
    return lax.dot_general(a, b, CONTRACT_LAST, preferred_element_type=F32)


def kernel(
    rhs_ref, root_ref, fwd_ref, coup_ref, rinv_ref, back_ref, bwd_ref, rows_ref,
    both_ref,
    rhs_v, fwd_v, coup_v, rinv_v, back_v, bwd_v, root_v, rows_v,
    part_f, part_b, core_in, x_f, x_out, x_in, rs_in, ag, y_keep,
    u_f, u_b, u_in, u_all, place, pick, p_rhs,
    xp_f, xp_b, xp_in, xr_all, rb_all, sel_out, sel_in, sel_all,
    z_out, a_f, b_f, a_in, b_in, a_out, b_out, fa_in, fb_in, own_f, own_in, flip, flip2,
    load_sem, core_s, core_r, xs_s, xs_r, rs_s, rs_r, ag_s, ag_r,
    us_s, us_r, za_s, za_r, pr_s, pr_r, ya_s, ya_r, xc_s, xc_r, xo_s, xo_r,
    rb_s, rb_r, se_s, se_r, pl_s, pl_r, a_s, a_r, b_s, b_r, fa_s, fa_r, fb_s, fb_r, end_s, end_r, w_s, w_r,
):
    l, r, q = lax.axis_index("leaf"), lax.axis_index("row"), lax.axis_index("col")
    x, h = q // 2, q % 2
    sib = (l, r, x * 2 + 1 - h)

    def xat(d):
        return lax.rem(x + d, 4)

    def yat(d):
        return lax.rem(r + d, 4)

    def zat(d):
        return lax.rem(l + d, 8)

    def load(src, dst, k):
        c = pltpu.make_async_copy(src, dst, load_sem.at[k])
        c.start()
        return c

    pending = []

    def send(src, dst, ss, rs, device):
        c = pltpu.make_async_remote_copy(
            src_ref=src, dst_ref=dst, send_sem=ss, recv_sem=rs, device_id=device, device_id_type=MESH
        )
        c.start()
        pending.append(c)

    def arrive(dst, ss, rs):
        pltpu.make_async_remote_copy(
            src_ref=dst, dst_ref=dst, send_sem=ss, recv_sem=rs, device_id=sib, device_id_type=MESH
        ).wait_recv()

    def flush():
        while pending:
            pending.pop(0).wait_send()

    l_rhs = load(rhs_ref, rhs_v, 0)
    l_fwd = []
    for j, d in enumerate(X_BLOCKS):
        cols = pl.ds(pl.multiple_of(xat(d) * 384, 128), 384)
        l_fwd.append(load(fwd_ref.at[:, cols], fwd_v.at[j], 1 + j))
    partners = [(l, r, xat(dx) * 2 + lax.rem(h + dh, 2)) for dx, dh in COL]
    partners += [(l, yat(dy), xat(dx) * 2 + h) for dy, dx in PLANE if dy]
    partners += [(l, yat(d), x * 2 + 1 - h) for d in Y_ORDER]
    partners += [(zat(d), r, q) for d in Z_ORDER]
    bar = pltpu.get_barrier_semaphore()
    for p in partners:
        pl.semaphore_signal(bar, inc=1, device_id=p, device_id_type=MESH)

    l_coup = load(coup_ref, coup_v.at[h], 6)
    l_rows = load(rows_ref, rows_v.at[l], 5)

    mine = pl.ds(pl.multiple_of(h * 64, 64), 64)
    other = pl.ds(pl.multiple_of((1 - h) * 64, 64), 64)
    l_rhs.wait()
    for j in range(4):
        l_fwd[j].wait()
        value = dot(rhs_v[...], fwd_v[j])
        part_f[j] = value
        part_b[j] = value.astype(BF)
        if j == 0:
            pl.semaphore_wait(bar, len(partners))
        send(part_b.at[j, other], core_in.at[j], core_s.at[j], core_r.at[j], sib)
    l_root = [
        load(root_ref.at[pl.ds(pl.multiple_of(g * 64 + r * 16, 16), 16)], root_v.at[pl.ds(g * 16, 16)], 11 + g)
        for g in range(2)
    ]
    l_rinv = load(rinv_ref, rinv_v, 8)
    l_back = load(back_ref, back_v.at[h], 9)
    l_bwd = load(bwd_ref, bwd_v.at[h], 10)
    l_coup.wait()
    send(coup_v.at[h], coup_v.at[h], w_s.at[2], w_r.at[2], sib)
    for j, d in enumerate(X_BLOCKS):
        arrive(core_in.at[j], core_s.at[j], core_r.at[j])
        both = part_f[j, mine, :] + core_in[j].astype(F32)
        x_f[j] = both
        x_out[j] = both.astype(BF)
        if d:
            send(x_out.at[j, 32:64], rs_in.at[j], rs_s.at[j], rs_r.at[j], (l, r, xat(d) * 2 + h))
    for j, d in enumerate(X_BLOCKS):
        for i, e in enumerate(X_ORDER):
            block = xat(d)
            send(x_out.at[j, 0:32], x_in.at[i, block], xs_s.at[i, j], xs_r.at[i, block], (l, r, xat(e) * 2 + h))

    l_rows.wait()
    for j, d in enumerate(Z_ORDER):
        send(rows_ref, rows_v.at[l], pr_s.at[j], pr_r.at[j], (zat(d), r, q))

    def build_place(leaf):
        row = rows_v[leaf, :, pl.ds(pl.multiple_of(q * 512, 512), 512)] - q * 1536

        @pl.loop(0, 12)
        def _(t):
            at = lax.broadcasted_iota(jnp.int32, (128, 512), 0) + t * 128
            place[leaf, pl.ds(pl.multiple_of(t * 128, 128), 128), :] = (at == row).astype(F32).astype(BF)

    def build_pick(leaf):
        row = rows_v[leaf, :, pl.ds(pl.multiple_of(l * 512 + r * 128, 128), 128)] - l * 1536

        @pl.loop(0, 12)
        def _(t):
            at = lax.broadcasted_iota(jnp.int32, (128, 128), 0) + t * 128
            pick[leaf, pl.ds(pl.multiple_of(t * 128, 128), 128), :] = (at == row).astype(F32).astype(BF)

    def rows_arrive(d):
        j = Z_ORDER.index((8 - d) % 8)
        arrive(rows_v.at[zat(d)], pr_s.at[j], pr_r.at[j])

    build_place(l)

    total = x_f[3, 32:64, :]
    for i in range(3):
        arrive(rs_in.at[i], rs_s.at[i], rs_r.at[i])
        total = total + rs_in[i].astype(F32)
    y_keep[32:64, :] = total
    ag[x] = total.astype(BF)
    for i, e in enumerate(X_ORDER):
        send(ag.at[x], ag.at[x], ag_s.at[i], ag_r.at[i], (l, r, xat(e) * 2 + h))
    for d in (1, 7, 2, 6):
        rows_arrive(d)
        build_place(zat(d))

    arrive(coup_v.at[1 - h], w_s.at[2], w_r.at[2])
    update = [jnp.zeros((64, 512), F32) for _ in range(2)]
    for d in (0, 1, 3, 2):
        block = xat(d)
        total = x_f[X_BLOCKS.index(d), 0:32, :]
        for i in range(3):
            arrive(x_in.at[i, block], xs_s.at[i, 0], xs_r.at[i, block])
            total = total + x_in[i, block].astype(F32)
        if d:
            i = X_ORDER.index((4 - d) % 4)
            arrive(ag.at[block], ag_s.at[i], ag_r.at[i])
        else:
            y_keep[0:32, :] = total
        left = jnp.concatenate([total.astype(BF), ag[block]], axis=0)
        for g in range(2):
            update[g] = update[g] + dot(left, coup_v[g, pl.ds(pl.multiple_of(block * 384, 128), 384), :])

    for g in range(2):
        u_f[g] = update[g]
        u_b[g] = update[g].astype(BF)
    for g in (0, 1):
        core = lax.rem(h + g, 2)
        for i, d in enumerate(Y_ORDER + ((0,) if g else ())):
            k = pl.ds(pl.multiple_of(yat(d) * 16, 16), 16)
            send(
                u_b.at[core, k], u_in.at[g, i], us_s.at[g, i], us_r.at[g, i], (l, yat(d), x * 2 + core)
            )
    l_back.wait()
    l_bwd.wait()
    send(back_v.at[h], back_v.at[h], w_s.at[0], w_r.at[0], sib)
    send(bwd_v.at[h], bwd_v.at[h], w_s.at[1], w_r.at[1], sib)
    for d in (3, 5, 4):
        rows_arrive(d)
        build_place(zat(d))
    total = u_f[h, pl.ds(pl.multiple_of(r * 16, 16), 16), :]
    for i in range(3):
        arrive(u_in.at[0, i], us_s.at[0, i], us_r.at[0, i])
        total = total + u_in[0, i].astype(F32)
    u_all[l, pl.ds(pl.multiple_of(h * 16, 16), 16), :] = total.astype(BF)
    total = jnp.zeros((16, 512), F32)
    for i in range(4):
        arrive(u_in.at[1, i], us_s.at[1, i], us_r.at[1, i])
        total = total + u_in[1, i].astype(F32)
    u_all[l, pl.ds(pl.multiple_of((1 - h) * 16, 16), 16), :] = total.astype(BF)

    for j, d in enumerate(Z_ORDER):
        send(u_all.at[l], u_all.at[l], za_s.at[j], za_r.at[j], (zat(d), r, q))
    for c in l_root:
        c.wait()
    placed = root_v[...] - dot_last(u_all[l], place[l])
    for d in Z_ARRIVAL[:6]:
        j = Z_ORDER.index((8 - d) % 8)
        leaf = zat(d)
        arrive(u_all.at[leaf], za_s.at[j], za_r.at[j])
        placed = placed - dot_last(u_all[leaf], place[leaf])
    d = Z_ARRIVAL[6]
    leaf = zat(d)
    arrive(u_all.at[leaf], za_s.at[Z_ORDER.index((8 - d) % 8)], za_r.at[Z_ORDER.index((8 - d) % 8)])

    for t in range(2):
        cols = slice(t * 768, t * 768 + 768)
        p_rhs[t, r] = (placed[:, cols] - dot_last(u_all[leaf], place[leaf, cols, :])).astype(BF)
        for i, d in enumerate(Y_ORDER):
            send(p_rhs.at[t, r], p_rhs.at[t, r], ya_s.at[t, i], ya_r.at[t, i], (l, yat(d), q))
    for d in range(8):
        build_pick(zat(d))
    l_rinv.wait()
    value = jnp.zeros((128, 384), F32)
    for t in range(2):
        for i, d in enumerate(Y_ORDER):
            arrive(p_rhs.at[t, yat(4 - d)], ya_s.at[t, i], ya_r.at[t, i])
        value = value + dot(p_rhs[t].reshape(128, 768), rinv_v[pl.ds(t * 768, 768), :])

    xp_f[...] = value
    xp_b[...] = value.astype(BF)
    for j, (dx, dh) in enumerate(COL):
        tx, th = xat(dx), lax.rem(h + dh, 2)
        k = pl.ds(pl.multiple_of(tx * 32 + th * 16, 16), 16)
        send(xp_b.at[k], xp_in.at[j], xc_s.at[j], xc_r.at[j], (l, r, tx * 2 + th))
    own_k = pl.ds(pl.multiple_of(h * 64 + x * 16, 16), 16)
    total = xp_f[pl.ds(pl.multiple_of(x * 32 + h * 16, 16), 16), :]
    for j in range(7):
        arrive(xp_in.at[j], xc_s.at[j], xc_r.at[j])
        total = total + xp_in[j].astype(F32)
    rb_all[r] = total.astype(BF)

    for j, d in enumerate(Y_ORDER):
        send(rb_all.at[r], rb_all.at[r], rb_s.at[j], rb_r.at[j], (l, yat(d), q))
    xr_all[own_k, :] = total
    for j, (dx, dh) in enumerate(COL):
        send(xr_all.at[own_k], xr_all.at[own_k], xo_s.at[j], xo_r.at[j], (l, r, xat(dx) * 2 + lax.rem(h + dh, 2)))
    for j, d in enumerate(Y_ORDER):
        arrive(rb_all.at[yat(4 - d)], rb_s.at[j], rb_r.at[j])
    root_rows = jnp.concatenate([rb_all[t] for t in range(4)], axis=1)

    for d in Z_ORDER + (0,):
        child = zat(d)
        chosen = dot(root_rows, pick[child]).astype(BF)
        if d:
            j = Z_ORDER.index(d)
            sel_out[child] = chosen
            send(sel_out.at[child], sel_in.at[NEAR.index(8 - d)], se_s.at[j], se_r.at[j], (child, r, q))
        else:
            sel_in[0] = chosen
    for j, (dx, dh) in enumerate(COL):
        k = pl.ds(pl.multiple_of(lax.rem(h + dh, 2) * 64 + xat(4 - dx) * 16, 16), 16)
        arrive(xr_all.at[k], xo_s.at[j], xo_r.at[j])
    flip[...] = xr_all[...].T
    both_ref[0:48, :] = flip[pl.ds(pl.multiple_of(q * 48, 16), 48), :]

    for g, (low, high) in enumerate(GROUPS):
        for n in range(max(low, 1), high):
            j = Z_ORDER.index(8 - NEAR[n])
            arrive(sel_in.at[n], se_s.at[j], se_r.at[j])
        for j, (dy, dx) in enumerate(PLANE):
            send(
                sel_in.at[low:high], sel_all.at[r, x, low:high], pl_s.at[g, j], pl_r.at[g, j], (l, yat(dy), xat(dx) * 2 + h)
            )
        sel_all[r, x, low:high] = sel_in[low:high]
    arrive(back_v.at[1 - h], w_s.at[0], w_r.at[0])
    arrive(bwd_v.at[1 - h], w_s.at[1], w_r.at[1])
    corr = jnp.zeros((64, 384), F32)
    for g, (low, high) in enumerate(GROUPS):
        for dy in (0, 1, 3, 2):
            sr = yat(dy)
            for dx in (0, 1, 3, 2):
                if dy or dx:
                    j = PLANE.index(((4 - dy) % 4, (4 - dx) % 4))
                    arrive(sel_all.at[sr, xat(dx), low:high], pl_s.at[g, j], pl_r.at[g, j])
            left = jnp.concatenate([sel_all[sr, :, n].reshape(64, 128) for n in range(low, high)], axis=1)
            right = jnp.concatenate(
                [
                    back_v[:, :, pl.ds(pl.multiple_of(zat(NEAR[n]) * 512 + sr * 128, 128), 128)].reshape(384, 128)
                    for n in range(low, high)
                ],
                axis=1,
            )
            corr = corr + dot_last(left, right)
    reduced = (y_keep[...] - corr).astype(BF)

    for j, (dy, dx) in enumerate(OWNERS):
        cols = pl.ds(pl.multiple_of((yat(dy) * 4 + xat(dx)) * 384, 128), 384)
        value = dot(reduced, bwd_v[:, :, cols].reshape(384, 384))
        z_out[j] = value.astype(BF)
        if dx:
            send(z_out.at[j, 0:32], a_in.at[dy, dx - 1], a_s.at[dy, dx - 1], a_r.at[dy, dx - 1], (l, r, xat(dx) * 2 + h))
        else:
            a_f[dy] = value[0:32]
        if dy:
            send(z_out.at[j, 32:64], b_in.at[dx, dy - 1], b_s.at[dx, dy - 1], b_r.at[dx, dy - 1], (l, yat(dy), x * 2 + h))
        else:
            b_f[dx] = value[32:64]
    for c in pending[:-24]:
        c.wait_send()
    del pending[:-24]
    for d in (2, 1, 3, 0):
        for first, came, s_sem, r_sem, on, fin, fin_s, fin_r, at in (
            (a_f, a_in, a_s, a_r, a_out, fa_in, fa_s, fa_r, 0), (b_f, b_in, b_s, b_r, b_out, fb_in, fb_s, fb_r, 32)
        ):
            total = first[d]
            for i in range(3):
                arrive(came.at[d, i], s_sem.at[d, i], r_sem.at[d, i])
                total = total + came[d, i].astype(F32)
            if d:
                on[d - 1] = total.astype(BF)
                for g in range(2):
                    to = (l, r, xat(d) * 2 + g) if at else (l, yat(d), x * 2 + g)
                    send(on.at[d - 1, :, g * 128 : g * 128 + 256], fin.at[h, d - 1], fin_s.at[g, d - 1], fin_r.at[h, d - 1], to)
            else:
                own_f[at : at + 32, :] = total

    send(
        own_f.at[:, pl.ds(pl.multiple_of((1 - h) * 128, 128), 256)], own_in.at[h], end_s.at[0], end_r.at[0], sib
    )
    own_in[h] = own_f[:, pl.ds(pl.multiple_of(h * 128, 128), 256)]
    flush()
    arrive(own_in.at[1 - h], end_s.at[0], end_r.at[0])
    for d in (2, 1, 3):
        for fin, fin_s, fin_r, at in ((fa_in, fa_s, fa_r, 0), (fb_in, fb_s, fb_r, 32)):
            for c in range(2):
                arrive(fin.at[c, d - 1], fin_s.at[c, d - 1], fin_r.at[c, d - 1])
                own_in[c, at : at + 32] = own_in[c, at : at + 32] + fin[c, d - 1].astype(F32)
    flip2[...] = own_in[...].reshape(128, 256).T
    both_ref[48:240, :] = flip2[pl.ds(pl.multiple_of(h * 64, 64), 192), :]


def split(both_ref, xroot_ref, xchild_ref):
    xroot_ref[...] = both_ref[0:48, :]
    xchild_ref[...] = both_ref[48:240, :]


def local(
    rhs_child, rhs_root, fwd_child, coupling, root_inverse, back_child, bwd_child, parent_rows
):
    vm = pltpu.VMEM
    dma = pltpu.SemaphoreType.DMA
    scratch = [
        vm((128, 768), BF), vm((4, 768, 384), BF), vm((2, 1536, 512), BF), vm((1536, 384), BF),
        vm((2, 192, 4096), BF), vm((2, 192, 6144), BF), vm((32, 1536), F32), vm((8, 1, 4096), jnp.int32),
        vm((4, 128, 384), F32), vm((4, 128, 384), BF), vm((4, 64, 384), BF), vm((4, 64, 384), F32),
        vm((4, 64, 384), BF), vm((3, 4, 32, 384), BF), vm((3, 32, 384), BF), vm((4, 32, 384), BF), vm((64, 384), F32),
        vm((2, 64, 512), F32), vm((2, 64, 512), BF), vm((2, 4, 16, 512), BF), vm((8, 32, 512), BF),
        vm((8, 1536, 512), BF), vm((8, 1536, 128), BF), vm((2, 4, 32, 768), BF),
        vm((128, 384), F32), vm((128, 384), BF), vm((7, 16, 384), BF), vm((128, 384), F32),
        vm((4, 16, 384), BF), vm((8, 16, 128), BF), vm((8, 16, 128), BF), vm((4, 4, 8, 16, 128), BF),
        vm((16, 64, 384), BF), vm((4, 32, 384), F32), vm((4, 32, 384), F32),
        vm((4, 3, 32, 384), BF), vm((4, 3, 32, 384), BF), vm((3, 32, 384), BF), vm((3, 32, 384), BF),
        vm((2, 3, 32, 256), BF), vm((2, 3, 32, 256), BF), vm((64, 384), F32), vm((2, 64, 256), F32),
        vm((384, 128), F32), vm((256, 128), F32),
        dma((13,)),
    ]
    for n in (4, (3, 4), 3, 3, (2, 4), 7, 7, (2, 3), 7, 7, 3, 7, (2, 15), (4, 3), (4, 3), (2, 3), (2, 3), 1, 3):
        n = n if isinstance(n, tuple) else (n,)
        scratch += [dma(n), dma(n)]
    any_spec = pl.BlockSpec(memory_space=pl.ANY)
    vm_spec = pl.BlockSpec(memory_space=pltpu.VMEM)
    both = pl.pallas_call(
        kernel,
        out_shape=pltpu.VMEM((240, 128), F32),
        in_specs=[any_spec] * 8,
        out_specs=vm_spec,
        scratch_shapes=scratch,
        compiler_params=pltpu.CompilerParams(
            collective_id=0, has_side_effects=True, vmem_limit_bytes=56 * 2**20
        ),
    )(
        rhs_child[0], rhs_root, fwd_child[0], coupling[0], root_inverse, back_child[0].T, bwd_child[0], parent_rows
    )
    x_root, x_child = pl.pallas_call(
        split,
        out_shape=(jax.ShapeDtypeStruct((48, 128), F32), jax.ShapeDtypeStruct((192, 128), F32)),
        in_specs=[vm_spec],
        out_specs=(vm_spec, vm_spec),
    )(pltpu.with_memory_space_constraint(both, pltpu.VMEM))
    return (x_root.T, x_child.T[None])


def solution(mesh):
    placed = (
        P("leaf", None, "col"),
        P(None, "col"),
        P("leaf", "col", "row"),
        P("leaf", "row", "col"),
        P("col", ("leaf", "row")),
        P("leaf", None, ("row", "col")),
        P("leaf", ("row", "col"), None),
        P("leaf", None),
    )
    return jax.shard_map(
        local,
        mesh=mesh,
        in_specs=placed,
        out_specs=(P(None, ("leaf", "row", "col")), P("leaf", None, ("row", "col"))),
        check_vma=False,
    )
```

```python
import jax
import jax.numpy as jnp
from jax import lax
from jax.experimental import pallas as pl
from jax.experimental.pallas import tpu as pltpu
from jax.sharding import PartitionSpec as P

BF = jnp.bfloat16
F32 = jnp.float32
MESH = pl.DeviceIdType.MESH
CONTRACT_LAST = (((1,), (1,)), ((), ()))

X_ORDER = (2, 1, 3)
NEAR = (0, 1, 7, 2, 6, 3, 5, 4)
GROUPS = ((0, 5), (5, 8))
SLOTS = 40
X_BLOCKS = X_ORDER + (0,)
Y_ORDER = (2, 1, 3)
Z_ORDER = (4, 3, 5, 2, 6, 1, 7)
Z_ARRIVAL = (4, 3, 5, 2, 6, 1, 7)
PLANE = sorted(
    ((dy, dx) for dy in range(4) for dx in range(4) if (dy, dx) != (0, 0)),
    key=lambda p: -(min(p[0], 4 - p[0]) + min(p[1], 4 - p[1])),
)
OWNERS = (
    (2, 2), (2, 1), (1, 2), (2, 3), (3, 2), (2, 0), (0, 2),
    (1, 1), (1, 3), (3, 1), (1, 0), (0, 1), (3, 3), (3, 0), (0, 3), (0, 0),
)
COL = [(dx, dh) for dx in (2, 1, 3) for dh in (1, 0)] + [(0, 1)]


def dot(a, b):
    return jnp.dot(a, b, preferred_element_type=F32)


def dot_last(a, b):
    return lax.dot_general(a, b, CONTRACT_LAST, preferred_element_type=F32)


def kernel(
    rhs_ref, root_ref, fwd_ref, coup_ref, rinv_ref, back_ref, bwd_ref, rows_ref,
    both_ref,
    rhs_v, fwd_v, coup_v, rinv_v, back_v, bwd_v, root_v, rows_v,
    part_f, part_b, core_in, x_f, x_out, x_in, rs_in, ag, y_keep,
    u_f, u_b, u_in, u_all, place, pick, p_rhs,
    xp_f, xp_b, xp_in, xr_all, rb_all, sel_out, sel_in, sel_all,
    z_out, a_f, b_f, a_in, b_in, a_out, b_out, fa_in, fb_in, own_f, own_in, flip, flip2,
    load_sem, send_sem, core_r, rs_r, xs_r, ag_r, pr_r, w_r, us_r, za_r, ya_r, xc_r, xo_r, rb_r, se_r, pl_r,
    a_r, b_r, fa_r, fb_r, end_r,
):
    l, r, q = lax.axis_index("leaf"), lax.axis_index("row"), lax.axis_index("col")
    x, h = q // 2, q % 2
    sib = (l, r, x * 2 + 1 - h)

    def xat(d):
        return lax.rem(x + d, 4)

    def yat(d):
        return lax.rem(r + d, 4)

    def zat(d):
        return lax.rem(l + d, 8)

    def load(src, dst, k):
        c = pltpu.make_async_copy(src, dst, load_sem.at[k])
        c.start()
        return c

    pending = []
    count = [0]

    def send(src, dst, rs, device):
        if len(pending) == SLOTS:
            pending.pop(0).wait_send()
        c = pltpu.make_async_remote_copy(
            src_ref=src, dst_ref=dst, send_sem=send_sem.at[count[0] % SLOTS], recv_sem=rs, device_id=device, device_id_type=MESH
        )
        c.start()
        count[0] += 1
        pending.append(c)

    def arrive(dst, rs):
        pltpu.make_async_remote_copy(
            src_ref=dst, dst_ref=dst, send_sem=send_sem.at[0], recv_sem=rs, device_id=sib, device_id_type=MESH
        ).wait_recv()

    def flush():
        while pending:
            pending.pop(0).wait_send()

    partners = [(l, r, xat(dx) * 2 + lax.rem(h + dh, 2)) for dx, dh in COL]
    partners += [(l, yat(dy), xat(dx) * 2 + h) for dy, dx in PLANE if dy]
    partners += [(l, yat(d), x * 2 + 1 - h) for d in Y_ORDER]
    partners += [(zat(d), r, q) for d in Z_ORDER[::-1]]
    bar = pltpu.get_barrier_semaphore()
    for p in partners[::-1]:
        pl.semaphore_signal(bar, inc=1, device_id=p, device_id_type=MESH)

    l_rhs = load(rhs_ref, rhs_v, 0)
    l_fwd = []
    for j, d in enumerate(X_BLOCKS):
        cols = pl.ds(pl.multiple_of(xat(d) * 384, 128), 384)
        l_fwd.append(load(fwd_ref.at[:, cols], fwd_v.at[j], 1 + j))
    l_coup = load(coup_ref, coup_v.at[h], 6)
    l_rows = load(rows_ref, rows_v.at[l], 5)

    l_rhs.wait()
    for j in range(4):
        l_fwd[j].wait()
        value = dot(rhs_v[...], fwd_v[j])
        part_f[j] = value
        part_b[j] = value.astype(BF)
        if j == 0:
            pl.semaphore_wait(bar, len(partners))
        for g in range(2):
            core = lax.rem(h + g, 2)
            if X_BLOCKS[j] or g:
                send(
                    part_b.at[j, pl.ds(pl.multiple_of(core * 64 + 32, 32), 32)], rs_in.at[min(2 * j + g, 6)], rs_r.at[0],
                    (l, r, xat(X_BLOCKS[j]) * 2 + core),
                )
        send(part_b.at[j, pl.ds(pl.multiple_of(64 - h * 64, 32), 32)], core_in.at[j], core_r.at[j], sib)
    l_root = [
        load(root_ref.at[pl.ds(pl.multiple_of(g * 64 + r * 16, 16), 16)], root_v.at[pl.ds(g * 16, 16)], 11 + g)
        for g in range(2)
    ]
    l_rinv = load(rinv_ref, rinv_v, 8)
    l_back = load(back_ref, back_v.at[h], 9)
    l_bwd = load(bwd_ref, bwd_v.at[h], 10)
    l_coup.wait()
    send(coup_v.at[h], coup_v.at[h], w_r.at[2], sib)
    for j, d in enumerate(X_BLOCKS):
        arrive(core_in.at[j], core_r.at[j])
        both = part_f[j, pl.ds(pl.multiple_of(h * 64, 32), 32), :] + core_in[j].astype(F32)
        x_f[j] = both
        x_out[j] = both.astype(BF)
        for i, e in enumerate(X_ORDER):
            block = xat(d)
            send(x_out.at[j], x_in.at[block, i], xs_r.at[block], (l, r, xat(e) * 2 + h))

    l_rows.wait()
    for j, d in enumerate(Z_ORDER):
        send(rows_ref, rows_v.at[l], pr_r.at[j], (zat(d), r, q))

    def build_place(leaf):
        row = rows_v[leaf, :, pl.ds(pl.multiple_of(q * 512, 512), 512)] - q * 1536

        @pl.loop(0, 12)
        def _(t):
            at = lax.broadcasted_iota(jnp.int32, (128, 512), 0) + t * 128
            place[leaf, pl.ds(pl.multiple_of(t * 128, 128), 128), :] = (at == row).astype(F32).astype(BF)

    def build_pick(leaf):
        row = rows_v[leaf, :, pl.ds(pl.multiple_of(l * 512 + r * 128, 128), 128)] - l * 1536

        @pl.loop(0, 12)
        def _(t):
            at = lax.broadcasted_iota(jnp.int32, (128, 128), 0) + t * 128
            pick[leaf, pl.ds(pl.multiple_of(t * 128, 128), 128), :] = (at == row).astype(F32).astype(BF)

    def rows_arrive(d):
        j = Z_ORDER.index((8 - d) % 8)
        arrive(rows_v.at[zat(d)], pr_r.at[j])

    build_place(l)

    total = part_f[3, pl.ds(pl.multiple_of(h * 64 + 32, 32), 32), :]
    arrive(rs_in, rs_r.at[0])
    for i in range(7):
        total = total + rs_in[i].astype(F32)
    y_keep[32:64, :] = total
    ag[x] = total.astype(BF)
    for i, e in enumerate(X_ORDER):
        send(ag.at[x], ag.at[x], ag_r.at[i], (l, r, xat(e) * 2 + h))
    for d in (1, 7, 2, 6):
        rows_arrive(d)
        build_place(zat(d))

    arrive(coup_v.at[1 - h], w_r.at[2])
    update = [jnp.zeros((64, 512), F32) for _ in range(2)]
    for d in (0, 1, 3, 2):
        block = xat(d)
        total = x_f[X_BLOCKS.index(d)]
        arrive(x_in.at[block], xs_r.at[block])
        for i in range(3):
            total = total + x_in[block, i].astype(F32)
        if d:
            i = X_ORDER.index((4 - d) % 4)
            arrive(ag.at[block], ag_r.at[i])
        else:
            y_keep[0:32, :] = total
        left = jnp.concatenate([total.astype(BF), ag[block]], axis=0)
        for g in range(2):
            update[g] = update[g] + dot(left, coup_v[g, pl.ds(pl.multiple_of(block * 384, 128), 384), :])

    for g in range(2):
        u_f[g] = update[g]
        u_b[g] = update[g].astype(BF)
    for g in (0, 1):
        core = lax.rem(h + g, 2)
        for i, d in enumerate(Y_ORDER + ((0,) if g else ())):
            k = pl.ds(pl.multiple_of(yat(d) * 16, 16), 16)
            send(
                u_b.at[core, k], u_in.at[g, i], us_r.at[g], (l, yat(d), x * 2 + core)
            )
    l_back.wait()
    l_bwd.wait()
    send(back_v.at[h], back_v.at[h], w_r.at[0], sib)
    send(bwd_v.at[h], bwd_v.at[h], w_r.at[1], sib)
    for d in (3, 5, 4):
        rows_arrive(d)
        build_place(zat(d))
    total = u_f[h, pl.ds(pl.multiple_of(r * 16, 16), 16), :]
    arrive(u_in.at[0, 0:3], us_r.at[0])
    for i in range(3):
        total = total + u_in[0, i].astype(F32)
    u_all[l, pl.ds(pl.multiple_of(h * 16, 16), 16), :] = total.astype(BF)
    total = jnp.zeros((16, 512), F32)
    arrive(u_in.at[1], us_r.at[1])
    for i in range(4):
        total = total + u_in[1, i].astype(F32)
    u_all[l, pl.ds(pl.multiple_of((1 - h) * 16, 16), 16), :] = total.astype(BF)

    for j, d in enumerate(Z_ORDER):
        send(u_all.at[l], u_all.at[l], za_r.at[j], (zat(d), r, q))
    for c in l_root:
        c.wait()
    placed = root_v[...] - dot_last(u_all[l], place[l])
    for d in Z_ARRIVAL[:6]:
        j = Z_ORDER.index((8 - d) % 8)
        leaf = zat(d)
        arrive(u_all.at[leaf], za_r.at[j])
        placed = placed - dot_last(u_all[leaf], place[leaf])
    d = Z_ARRIVAL[6]
    leaf = zat(d)
    arrive(u_all.at[leaf], za_r.at[Z_ORDER.index((8 - d) % 8)])

    for t in range(3):
        cols = slice(t * 512, t * 512 + 512)
        p_rhs[t, r] = (placed[:, cols] - dot_last(u_all[leaf], place[leaf, cols, :])).astype(BF)
        for i, d in enumerate(Y_ORDER):
            send(p_rhs.at[t, r], p_rhs.at[t, r], ya_r.at[t], (l, yat(d), q))
    for d in range(8):
        build_pick(zat(d))
    l_rinv.wait()
    value = jnp.zeros((128, 384), F32)
    for t in range(3):
        arrive(p_rhs.at[t, 0:3], ya_r.at[t])
        value = value + dot(p_rhs[t].reshape(128, 512), rinv_v[pl.ds(t * 512, 512), :])

    xp_f[...] = value
    xp_b[...] = value.astype(BF)
    for j, (dx, dh) in enumerate(COL):
        tx, th = xat(dx), lax.rem(h + dh, 2)
        k = pl.ds(pl.multiple_of(tx * 32 + th * 16, 16), 16)
        send(xp_b.at[k], xp_in.at[j], xc_r.at[0], (l, r, tx * 2 + th))
    own_k = pl.ds(pl.multiple_of(h * 64 + x * 16, 16), 16)
    total = xp_f[pl.ds(pl.multiple_of(x * 32 + h * 16, 16), 16), :]
    arrive(xp_in, xc_r.at[0])
    for j in range(7):
        total = total + xp_in[j].astype(F32)
    rb_all[r] = total.astype(BF)

    for d in Y_ORDER:
        send(rb_all.at[r], rb_all.at[r], rb_r.at[0], (l, yat(d), q))
    xr_all[own_k, :] = total
    for j, (dx, dh) in enumerate(COL):
        send(xr_all.at[own_k], xr_all.at[own_k], xo_r.at[0], (l, r, xat(dx) * 2 + lax.rem(h + dh, 2)))
    arrive(rb_all.at[0:3], rb_r.at[0])
    root_rows = jnp.concatenate([rb_all[t] for t in range(4)], axis=1)

    for d in Z_ORDER + (0,):
        child = zat(d)
        chosen = dot(root_rows, pick[child]).astype(BF)
        if d:
            n = NEAR.index(8 - d)
            sel_out[child] = chosen
            send(sel_out.at[child], sel_in.at[n], se_r.at[0 if n < GROUPS[0][1] else 1], (child, r, q))
        else:
            sel_in[0] = chosen
    arrive(xr_all.at[0:112], xo_r.at[0])
    flip[...] = xr_all[...].T
    both_ref[0:48, :] = flip[pl.ds(pl.multiple_of(q * 48, 16), 48), :]

    for g, (low, high) in enumerate(GROUPS):
        arrive(sel_in.at[max(low, 1) : high], se_r.at[g])
        for dy, dx in PLANE:
            send(
                sel_in.at[low:high], sel_all.at[r, x, low:high], pl_r.at[g, dy], (l, yat(dy), xat(dx) * 2 + h)
            )
        sel_all[r, x, low:high] = sel_in[low:high]
    arrive(back_v.at[1 - h], w_r.at[0])
    arrive(bwd_v.at[1 - h], w_r.at[1])
    corr = jnp.zeros((64, 384), F32)
    for g, (low, high) in enumerate(GROUPS):
        for dy in (0, 1, 3, 2):
            sr = yat(dy)
            arrive(sel_all.at[sr, 0 : 4 if dy else 3, low:high], pl_r.at[g, (4 - dy) % 4])
            left = jnp.concatenate([sel_all[sr, :, n].reshape(64, 128) for n in range(low, high)], axis=1)
            right = jnp.concatenate(
                [
                    back_v[:, :, pl.ds(pl.multiple_of(zat(NEAR[n]) * 512 + sr * 128, 128), 128)].reshape(384, 128)
                    for n in range(low, high)
                ],
                axis=1,
            )
            corr = corr + dot_last(left, right)
    reduced = (y_keep[...] - corr).astype(BF)

    for j, (dy, dx) in enumerate(OWNERS):
        cols = pl.ds(pl.multiple_of((yat(dy) * 4 + xat(dx)) * 384, 128), 384)
        value = dot(reduced, bwd_v[:, :, cols].reshape(384, 384))
        z_out[j] = value.astype(BF)
        if dx:
            send(z_out.at[j, 0:32], a_in.at[dy, dx - 1], a_r.at[dy], (l, r, xat(dx) * 2 + h))
        else:
            a_f[dy] = value[0:32]
        if dy:
            send(z_out.at[j, 32:64], b_in.at[dx, dy - 1], b_r.at[dx], (l, yat(dy), x * 2 + h))
        else:
            b_f[dx] = value[32:64]
    for c in pending[:-24]:
        c.wait_send()
    del pending[:-24]
    for d in (2, 1, 3, 0):
        for first, came, came_r, on, fin, fin_r, at in (
            (a_f, a_in, a_r, a_out, fa_in, fa_r, 0), (b_f, b_in, b_r, b_out, fb_in, fb_r, 32)
        ):
            total = first[d]
            arrive(came.at[d], came_r.at[d])
            for i in range(3):
                total = total + came[d, i].astype(F32)
            if d:
                on[d - 1] = total.astype(BF)
                for g in range(2):
                    to = (l, r, xat(d) * 2 + g) if at else (l, yat(d), x * 2 + g)
                    send(on.at[d - 1, :, g * 128 : g * 128 + 256], fin.at[d - 1, h], fin_r.at[d - 1], to)
            else:
                own_f[at : at + 32, :] = total

    send(
        own_f.at[:, pl.ds(pl.multiple_of((1 - h) * 128, 128), 256)], own_in.at[h], end_r.at[0], sib
    )
    own_in[h] = own_f[:, pl.ds(pl.multiple_of(h * 128, 128), 256)]
    flush()
    arrive(own_in.at[1 - h], end_r.at[0])
    for d in (2, 1, 3):
        for fin, fin_r, at in ((fa_in, fa_r, 0), (fb_in, fb_r, 32)):
            arrive(fin.at[d - 1], fin_r.at[d - 1])
            for c in range(2):
                own_in[c, at : at + 32] = own_in[c, at : at + 32] + fin[d - 1, c].astype(F32)
    flip2[...] = own_in[...].reshape(128, 256).T
    both_ref[48:240, :] = flip2[pl.ds(pl.multiple_of(h * 64, 64), 192), :]


def split(both_ref, xroot_ref, xchild_ref):
    xroot_ref[...] = both_ref[0:48, :]
    xchild_ref[...] = both_ref[48:240, :]


def local(
    rhs_child, rhs_root, fwd_child, coupling, root_inverse, back_child, bwd_child, parent_rows
):
    vm = pltpu.VMEM
    dma = pltpu.SemaphoreType.DMA
    scratch = [
        vm((128, 768), BF), vm((4, 768, 384), BF), vm((2, 1536, 512), BF), vm((1536, 384), BF),
        vm((2, 192, 4096), BF), vm((2, 192, 6144), BF), vm((32, 1536), F32), vm((8, 1, 4096), jnp.int32),
        vm((4, 128, 384), F32), vm((4, 128, 384), BF), vm((4, 32, 384), BF), vm((4, 32, 384), F32),
        vm((4, 32, 384), BF), vm((4, 3, 32, 384), BF), vm((7, 32, 384), BF), vm((4, 32, 384), BF), vm((64, 384), F32),
        vm((2, 64, 512), F32), vm((2, 64, 512), BF), vm((2, 4, 16, 512), BF), vm((8, 32, 512), BF),
        vm((8, 1536, 512), BF), vm((8, 1536, 128), BF), vm((3, 4, 32, 512), BF),
        vm((128, 384), F32), vm((128, 384), BF), vm((7, 16, 384), BF), vm((128, 384), F32),
        vm((4, 16, 384), BF), vm((8, 16, 128), BF), vm((8, 16, 128), BF), vm((4, 4, 8, 16, 128), BF),
        vm((16, 64, 384), BF), vm((4, 32, 384), F32), vm((4, 32, 384), F32),
        vm((4, 3, 32, 384), BF), vm((4, 3, 32, 384), BF), vm((3, 32, 384), BF), vm((3, 32, 384), BF),
        vm((3, 2, 32, 256), BF), vm((3, 2, 32, 256), BF), vm((64, 384), F32), vm((2, 64, 256), F32),
        vm((384, 128), F32), vm((256, 128), F32),
        dma((13,)), dma((SLOTS,)),
    ]
    for n in (4, 1, 4, 3, 7, 3, 2, 7, 3, 1, 1, 1, 2, (2, 4), 4, 4, 3, 3, 1):
        scratch.append(dma(n if isinstance(n, tuple) else (n,)))
    any_spec = pl.BlockSpec(memory_space=pl.ANY)
    vm_spec = pl.BlockSpec(memory_space=pltpu.VMEM)
    both = pl.pallas_call(
        kernel,
        out_shape=pltpu.VMEM((240, 128), F32),
        in_specs=[any_spec] * 8,
        out_specs=vm_spec,
        scratch_shapes=scratch,
        compiler_params=pltpu.CompilerParams(
            collective_id=0, has_side_effects=True, vmem_limit_bytes=56 * 2**20
        ),
    )(
        rhs_child[0], rhs_root, fwd_child[0], coupling[0], root_inverse, back_child[0].T, bwd_child[0], parent_rows
    )
    x_root, x_child = pl.pallas_call(
        split,
        out_shape=(jax.ShapeDtypeStruct((48, 128), F32), jax.ShapeDtypeStruct((192, 128), F32)),
        in_specs=[vm_spec],
        out_specs=(vm_spec, vm_spec),
    )(pltpu.with_memory_space_constraint(both, pltpu.VMEM))
    return (x_root.T, x_child.T[None])


def solution(mesh):
    placed = (
        P("leaf", None, "col"),
        P(None, "col"),
        P("leaf", "col", "row"),
        P("leaf", "row", "col"),
        P("col", ("leaf", "row")),
        P("leaf", None, ("row", "col")),
        P("leaf", ("row", "col"), None),
        P("leaf", None),
    )
    return jax.shard_map(
        local,
        mesh=mesh,
        in_specs=placed,
        out_specs=(P(None, ("leaf", "row", "col")), P("leaf", None, ("row", "col"))),
        check_vma=False,
    )
```

```python
import jax
import jax.numpy as jnp
from jax import lax
from jax.experimental import pallas as pl
from jax.experimental.pallas import tpu as pltpu
from jax.sharding import PartitionSpec as P

BF = jnp.bfloat16
F32 = jnp.float32
MESH = pl.DeviceIdType.MESH
CONTRACT_LAST = (((1,), (1,)), ((), ()))

X_ORDER = (2, 1, 3)
NEAR = (0, 1, 7, 2, 6, 3, 5, 4)
GROUPS = ((0, 5), (5, 8))
SLOTS = 24
X_BLOCKS = X_ORDER + (0,)
Y_ORDER = (2, 1, 3)
Z_ORDER = (4, 3, 5, 2, 6, 1, 7)
Z_ARRIVAL = (4, 3, 5, 2, 6, 1, 7)
PLANE = sorted(
    ((dy, dx) for dy in range(4) for dx in range(4) if (dy, dx) != (0, 0)),
    key=lambda p: -(min(p[0], 4 - p[0]) + min(p[1], 4 - p[1])),
)
OWNERS = (
    (2, 2), (2, 1), (1, 2), (2, 3), (3, 2), (2, 0), (0, 2),
    (1, 1), (1, 3), (3, 1), (1, 0), (0, 1), (3, 3), (3, 0), (0, 3), (0, 0),
)
COL = [(dx, dh) for dx in (2, 1, 3) for dh in (1, 0)] + [(0, 1)]


def dot(a, b):
    return jnp.dot(a, b, preferred_element_type=F32)


def dot_last(a, b):
    return lax.dot_general(a, b, CONTRACT_LAST, preferred_element_type=F32)


def kernel(
    rhs_ref, root_ref, fwd_ref, coup_ref, rinv_ref, back_ref, bwd_ref, rows_ref,
    both_ref,
    rhs_v, fwd_v, coup_v, rinv_v, back_v, bwd_v, root_v, rows_v,
    part_f, part_b, core_in, x_f, x_out, x_in, rs_in, ag, y_keep,
    u_f, u_b, u_in, u_all, place, pick, p_rhs,
    xp_f, xp_b, xp_in, xr_all, rb_all, sel_out, sel_in, sel_all,
    z_out, a_f, b_f, a_in, b_in, a_out, b_out, fa_in, fb_in, own_f, own_in, flip, flip2,
    load_sem, send_sem, core_r, rs_r, xs_r, ag_r, pr_r, w_r, us_r, za_r, ya_r, xc_r, xo_r, rb_r, se_r, pl_r,
    fa_r, fb_r, end_r,
):
    l, r, q = lax.axis_index("leaf"), lax.axis_index("row"), lax.axis_index("col")
    x, h = q // 2, q % 2
    sib = (l, r, x * 2 + 1 - h)

    def xat(d):
        return lax.rem(x + d, 4)

    def yat(d):
        return lax.rem(r + d, 4)

    def zat(d):
        return lax.rem(l + d, 8)

    def load(src, dst, k):
        c = pltpu.make_async_copy(src, dst, load_sem.at[k])
        c.start()
        return c

    pending = []
    count = [0]

    def send(src, dst, rs, device):
        if len(pending) == SLOTS:
            pending.pop(0).wait_send()
        c = pltpu.make_async_remote_copy(
            src_ref=src, dst_ref=dst, send_sem=send_sem.at[count[0] % SLOTS], recv_sem=rs, device_id=device, device_id_type=MESH
        )
        c.start()
        count[0] += 1
        pending.append(c)

    def arrive(dst, rs):
        pltpu.make_async_remote_copy(
            src_ref=dst, dst_ref=dst, send_sem=send_sem.at[0], recv_sem=rs, device_id=sib, device_id_type=MESH
        ).wait_recv()

    def flush():
        while pending:
            pending.pop(0).wait_send()

    partners = [(l, r, xat(dx) * 2 + lax.rem(h + dh, 2)) for dx, dh in COL]
    partners += [(l, yat(dy), xat(dx) * 2 + h) for dy, dx in PLANE if dy]
    partners += [(l, yat(d), x * 2 + 1 - h) for d in Y_ORDER]
    partners += [(zat(d), r, q) for d in Z_ORDER[::-1]]
    bar = pltpu.get_barrier_semaphore()
    for p in partners[::-1]:
        pl.semaphore_signal(bar, inc=1, device_id=p, device_id_type=MESH)

    l_rhs = load(rhs_ref, rhs_v, 0)
    l_fwd = []
    for j, d in enumerate(X_BLOCKS):
        cols = pl.ds(pl.multiple_of(xat(d) * 384, 128), 384)
        l_fwd.append(load(fwd_ref.at[:, cols], fwd_v.at[j], 1 + j))
    l_coup = load(coup_ref, coup_v.at[h], 6)
    l_rows = load(rows_ref, rows_v.at[l], 5)

    l_rhs.wait()
    for j in range(4):
        l_fwd[j].wait()
        value = dot(rhs_v[...], fwd_v[j])
        part_f[j] = value
        part_b[j] = value.astype(BF)
        if j == 0:
            pl.semaphore_wait(bar, len(partners))
        for g in range(2):
            core = lax.rem(h + g, 2)
            if X_BLOCKS[j] or g:
                send(
                    part_b.at[j, pl.ds(pl.multiple_of(core * 64 + 32, 32), 32)], rs_in.at[min(2 * j + g, 6)], rs_r.at[0],
                    (l, r, xat(X_BLOCKS[j]) * 2 + core),
                )
        send(part_b.at[j, pl.ds(pl.multiple_of(64 - h * 64, 32), 32)], core_in.at[j], core_r.at[j], sib)
    l_root = [
        load(root_ref.at[pl.ds(pl.multiple_of(g * 64 + r * 16, 16), 16)], root_v.at[pl.ds(g * 16, 16)], 11 + g)
        for g in range(2)
    ]
    l_rinv = load(rinv_ref, rinv_v, 8)
    l_back = load(back_ref, back_v.at[h], 9)
    l_bwd = load(bwd_ref, bwd_v.at[h], 10)
    l_coup.wait()
    send(coup_v.at[h], coup_v.at[h], w_r.at[2], sib)
    for j, d in enumerate(X_BLOCKS):
        arrive(core_in.at[j], core_r.at[j])
        both = part_f[j, pl.ds(pl.multiple_of(h * 64, 32), 32), :] + core_in[j].astype(F32)
        x_f[j] = both
        x_out[j] = both.astype(BF)
        for i, e in enumerate(X_ORDER):
            block = xat(d)
            send(x_out.at[j], x_in.at[block, i], xs_r.at[block], (l, r, xat(e) * 2 + h))

    l_rows.wait()
    for d in Z_ORDER:
        send(rows_ref, rows_v.at[l], pr_r.at[0 if d in (1, 7, 2, 6) else 1], (zat(d), r, q))

    def build_place(leaf):
        row = rows_v[leaf, :, pl.ds(pl.multiple_of(q * 512, 512), 512)] - q * 1536

        @pl.loop(0, 12)
        def _(t):
            at = lax.broadcasted_iota(jnp.int32, (128, 512), 0) + t * 128
            place[leaf, pl.ds(pl.multiple_of(t * 128, 128), 128), :] = (at == row).astype(F32).astype(BF)

    def build_pick(leaf):
        row = rows_v[leaf, :, pl.ds(pl.multiple_of(l * 512 + r * 128, 128), 128)] - l * 1536

        @pl.loop(0, 12)
        def _(t):
            at = lax.broadcasted_iota(jnp.int32, (128, 128), 0) + t * 128
            pick[leaf, pl.ds(pl.multiple_of(t * 128, 128), 128), :] = (at == row).astype(F32).astype(BF)

    build_place(l)

    total = part_f[3, pl.ds(pl.multiple_of(h * 64 + 32, 32), 32), :]
    arrive(rs_in, rs_r.at[0])
    for i in range(7):
        total = total + rs_in[i].astype(F32)
    y_keep[32:64, :] = total
    ag[x] = total.astype(BF)
    for i, e in enumerate(X_ORDER):
        send(ag.at[x], ag.at[x], ag_r.at[i], (l, r, xat(e) * 2 + h))
    arrive(rows_v.at[0:4], pr_r.at[0])
    for d in (1, 7, 2, 6):
        build_place(zat(d))

    arrive(coup_v.at[1 - h], w_r.at[2])
    update = [jnp.zeros((64, 512), F32) for _ in range(2)]
    for d in (0, 1, 3, 2):
        block = xat(d)
        total = x_f[X_BLOCKS.index(d)]
        arrive(x_in.at[block], xs_r.at[block])
        for i in range(3):
            total = total + x_in[block, i].astype(F32)
        if d:
            i = X_ORDER.index((4 - d) % 4)
            arrive(ag.at[block], ag_r.at[i])
        else:
            y_keep[0:32, :] = total
        left = jnp.concatenate([total.astype(BF), ag[block]], axis=0)
        rows = pl.ds(pl.multiple_of(block * 384, 128), 384)
        for g in range(2):
            core = lax.rem(h + g, 2)
            update[g] = update[g] + dot(left, coup_v[core, rows, :])
            if d == 2:
                u_b[g] = update[g].astype(BF)
                for i, e in enumerate(Y_ORDER + ((0,) if g else ())):
                    k = pl.ds(pl.multiple_of(yat(e) * 16, 16), 16)
                    send(u_b.at[g, k], u_in.at[g, i], us_r.at[g], (l, yat(e), x * 2 + core))
    u_f[...] = update[0]

    l_back.wait()
    l_bwd.wait()
    send(back_v.at[h], back_v.at[h], w_r.at[0], sib)
    send(bwd_v.at[h], bwd_v.at[h], w_r.at[1], sib)
    arrive(rows_v.at[0:3], pr_r.at[1])
    for d in (3, 5, 4):
        build_place(zat(d))
    total = u_f[pl.ds(pl.multiple_of(r * 16, 16), 16), :]
    arrive(u_in.at[0, 0:3], us_r.at[0])
    for i in range(3):
        total = total + u_in[0, i].astype(F32)
    u_all[l, pl.ds(pl.multiple_of(h * 16, 16), 16), :] = total.astype(BF)
    total = jnp.zeros((16, 512), F32)
    arrive(u_in.at[1], us_r.at[1])
    for i in range(4):
        total = total + u_in[1, i].astype(F32)
    u_all[l, pl.ds(pl.multiple_of((1 - h) * 16, 16), 16), :] = total.astype(BF)

    for j, d in enumerate(Z_ORDER):
        send(u_all.at[l], u_all.at[l], za_r.at[j], (zat(d), r, q))
    for c in l_root:
        c.wait()
    placed = root_v[...] - dot_last(u_all[l], place[l])
    for d in Z_ARRIVAL[:6]:
        j = Z_ORDER.index((8 - d) % 8)
        leaf = zat(d)
        arrive(u_all.at[leaf], za_r.at[j])
        placed = placed - dot_last(u_all[leaf], place[leaf])
    d = Z_ARRIVAL[6]
    leaf = zat(d)
    arrive(u_all.at[leaf], za_r.at[Z_ORDER.index((8 - d) % 8)])

    for t in range(3):
        cols = slice(t * 512, t * 512 + 512)
        p_rhs[t, r] = (placed[:, cols] - dot_last(u_all[leaf], place[leaf, cols, :])).astype(BF)
        for i, d in enumerate(Y_ORDER):
            send(p_rhs.at[t, r], p_rhs.at[t, r], ya_r.at[t], (l, yat(d), q))
    for d in range(8):
        build_pick(zat(d))
    l_rinv.wait()
    value = jnp.zeros((128, 384), F32)
    for t in range(3):
        arrive(p_rhs.at[t, 0:3], ya_r.at[t])
        value = value + dot(p_rhs[t].reshape(128, 512), rinv_v[pl.ds(t * 512, 512), :])

    xp_f[...] = value
    xp_b[...] = value.astype(BF)
    for j, (dx, dh) in enumerate(COL):
        tx, th = xat(dx), lax.rem(h + dh, 2)
        k = pl.ds(pl.multiple_of(tx * 32 + th * 16, 16), 16)
        send(xp_b.at[k], xp_in.at[j], xc_r.at[0], (l, r, tx * 2 + th))
    own_k = pl.ds(pl.multiple_of(h * 64 + x * 16, 16), 16)
    total = xp_f[pl.ds(pl.multiple_of(x * 32 + h * 16, 16), 16), :]
    arrive(xp_in, xc_r.at[0])
    for j in range(7):
        total = total + xp_in[j].astype(F32)
    rb_all[r] = total.astype(BF)

    for d in Y_ORDER:
        send(rb_all.at[r], rb_all.at[r], rb_r.at[0], (l, yat(d), q))
    xr_all[own_k, :] = total
    for j, (dx, dh) in enumerate(COL):
        send(xr_all.at[own_k], xr_all.at[own_k], xo_r.at[0], (l, r, xat(dx) * 2 + lax.rem(h + dh, 2)))
    arrive(rb_all.at[0:3], rb_r.at[0])
    root_rows = jnp.concatenate([rb_all[t] for t in range(4)], axis=1)

    for d in Z_ORDER + (0,):
        child = zat(d)
        chosen = dot(root_rows, pick[child]).astype(BF)
        if d:
            n = NEAR.index(8 - d)
            sel_out[child] = chosen
            send(sel_out.at[child], sel_in.at[n], se_r.at[0 if n < GROUPS[0][1] else 1], (child, r, q))
        else:
            sel_in[0] = chosen
    arrive(xr_all.at[0:112], xo_r.at[0])
    flip[...] = xr_all[...].T
    both_ref[0:48, :] = flip[pl.ds(pl.multiple_of(q * 48, 16), 48), :]

    for g, (low, high) in enumerate(GROUPS):
        arrive(sel_in.at[max(low, 1) : high], se_r.at[g])
        for dy, dx in PLANE:
            send(
                sel_in.at[low:high], sel_all.at[r, x, low:high], pl_r.at[g, dy], (l, yat(dy), xat(dx) * 2 + h)
            )
        sel_all[r, x, low:high] = sel_in[low:high]
    arrive(back_v.at[1 - h], w_r.at[0])
    arrive(bwd_v.at[1 - h], w_r.at[1])
    corr = jnp.zeros((64, 384), F32)
    for g, (low, high) in enumerate(GROUPS):
        for dy in (0, 1, 3, 2):
            sr = yat(dy)
            arrive(sel_all.at[sr, 0 : 4 if dy else 3, low:high], pl_r.at[g, (4 - dy) % 4])
            left = jnp.concatenate([sel_all[sr, :, n].reshape(64, 128) for n in range(low, high)], axis=1)
            right = jnp.concatenate(
                [
                    back_v[:, :, pl.ds(pl.multiple_of(zat(NEAR[n]) * 512 + sr * 128, 128), 128)].reshape(384, 128)
                    for n in range(low, high)
                ],
                axis=1,
            )
            corr = corr + dot_last(left, right)
    reduced = (y_keep[...] - corr).astype(BF)

    for j, (dy, dx) in enumerate(OWNERS):
        cols = pl.ds(pl.multiple_of((yat(dy) * 4 + xat(dx)) * 384, 128), 384)
        value = dot(reduced, bwd_v[:, :, cols].reshape(384, 384))
        z_out[j] = value.astype(BF)
        if dx:
            send(z_out.at[j, 0:32], a_in.at[dy, dx - 1], core_r.at[dy], (l, r, xat(dx) * 2 + h))
        else:
            a_f[dy] = value[0:32]
        if dy:
            send(z_out.at[j, 32:64], b_in.at[dx, dy - 1], xs_r.at[dx], (l, yat(dy), x * 2 + h))
        else:
            b_f[dx] = value[32:64]
    for c in pending[:-24]:
        c.wait_send()
    del pending[:-24]
    for d in (2, 1, 3, 0):
        for first, came, came_r, on, fin, fin_r, at in (
            (a_f, a_in, core_r, a_out, fa_in, fa_r, 0), (b_f, b_in, xs_r, b_out, fb_in, fb_r, 32)
        ):
            total = first[d]
            arrive(came.at[d], came_r.at[d])
            for i in range(3):
                total = total + came[d, i].astype(F32)
            if d:
                on[d - 1] = total.astype(BF)
                for g in range(2):
                    to = (l, r, xat(d) * 2 + g) if at else (l, yat(d), x * 2 + g)
                    send(on.at[d - 1, :, g * 128 : g * 128 + 256], fin.at[d - 1, h], fin_r.at[d - 1], to)
            else:
                own_f[at : at + 32, :] = total

    send(
        own_f.at[:, pl.ds(pl.multiple_of((1 - h) * 128, 128), 256)], own_in.at[h], end_r.at[0], sib
    )
    own_in[h] = own_f[:, pl.ds(pl.multiple_of(h * 128, 128), 256)]
    flush()
    arrive(own_in.at[1 - h], end_r.at[0])
    for d in (2, 1, 3):
        for fin, fin_r, at in ((fa_in, fa_r, 0), (fb_in, fb_r, 32)):
            arrive(fin.at[d - 1], fin_r.at[d - 1])
            for c in range(2):
                own_in[c, at : at + 32] = own_in[c, at : at + 32] + fin[d - 1, c].astype(F32)
    flip2[...] = own_in[...].reshape(128, 256).T
    both_ref[48:240, :] = flip2[pl.ds(pl.multiple_of(h * 64, 64), 192), :]


def split(both_ref, xroot_ref, xchild_ref):
    xroot_ref[...] = both_ref[0:48, :]
    xchild_ref[...] = both_ref[48:240, :]


def local(
    rhs_child, rhs_root, fwd_child, coupling, root_inverse, back_child, bwd_child, parent_rows
):
    vm = pltpu.VMEM
    dma = pltpu.SemaphoreType.DMA
    scratch = [
        vm((128, 768), BF), vm((4, 768, 384), BF), vm((2, 1536, 512), BF), vm((1536, 384), BF),
        vm((2, 192, 4096), BF), vm((2, 192, 6144), BF), vm((32, 1536), F32), vm((8, 1, 4096), jnp.int32),
        vm((4, 128, 384), F32), vm((4, 128, 384), BF), vm((4, 32, 384), BF), vm((4, 32, 384), F32),
        vm((4, 32, 384), BF), vm((4, 3, 32, 384), BF), vm((7, 32, 384), BF), vm((4, 32, 384), BF), vm((64, 384), F32),
        vm((64, 512), F32), vm((2, 64, 512), BF), vm((2, 4, 16, 512), BF), vm((8, 32, 512), BF),
        vm((8, 1536, 512), BF), vm((8, 1536, 128), BF), vm((3, 4, 32, 512), BF),
        vm((128, 384), F32), vm((128, 384), BF), vm((7, 16, 384), BF), vm((128, 384), F32),
        vm((4, 16, 384), BF), vm((8, 16, 128), BF), vm((8, 16, 128), BF), vm((4, 4, 8, 16, 128), BF),
        vm((16, 64, 384), BF), vm((4, 32, 384), F32), vm((4, 32, 384), F32),
        vm((4, 3, 32, 384), BF), vm((4, 3, 32, 384), BF), vm((3, 32, 384), BF), vm((3, 32, 384), BF),
        vm((3, 2, 32, 256), BF), vm((3, 2, 32, 256), BF), vm((64, 384), F32), vm((2, 64, 256), F32),
        vm((384, 128), F32), vm((256, 128), F32),
        dma((13,)), dma((SLOTS,)),
    ]
    for n in (4, 1, 4, 3, 2, 3, 2, 7, 3, 1, 1, 1, 2, (2, 4), 3, 3, 1):
        scratch.append(dma(n if isinstance(n, tuple) else (n,)))
    any_spec = pl.BlockSpec(memory_space=pl.ANY)
    vm_spec = pl.BlockSpec(memory_space=pltpu.VMEM)
    both = pl.pallas_call(
        kernel,
        out_shape=pltpu.VMEM((240, 128), F32),
        in_specs=[any_spec] * 8,
        out_specs=vm_spec,
        scratch_shapes=scratch,
        compiler_params=pltpu.CompilerParams(
            collective_id=0, has_side_effects=True, vmem_limit_bytes=56 * 2**20
        ),
    )(
        rhs_child[0], rhs_root, fwd_child[0], coupling[0], root_inverse, back_child[0].T, bwd_child[0], parent_rows
    )
    x_root, x_child = pl.pallas_call(
        split,
        out_shape=(jax.ShapeDtypeStruct((48, 128), F32), jax.ShapeDtypeStruct((192, 128), F32)),
        in_specs=[vm_spec],
        out_specs=(vm_spec, vm_spec),
    )(pltpu.with_memory_space_constraint(both, pltpu.VMEM))
    return (x_root.T, x_child.T[None])


def solution(mesh):
    placed = (
        P("leaf", None, "col"),
        P(None, "col"),
        P("leaf", "col", "row"),
        P("leaf", "row", "col"),
        P("col", ("leaf", "row")),
        P("leaf", None, ("row", "col")),
        P("leaf", ("row", "col"), None),
        P("leaf", None),
    )
    return jax.shard_map(
        local,
        mesh=mesh,
        in_specs=placed,
        out_specs=(P(None, ("leaf", "row", "col")), P("leaf", None, ("row", "col"))),
        check_vma=False,
    )
```

```python
import jax
import jax.numpy as jnp
from jax import lax
from jax.experimental import pallas as pl
from jax.experimental.pallas import tpu as pltpu
from jax.sharding import PartitionSpec as P

BF = jnp.bfloat16
F32 = jnp.float32
MESH = pl.DeviceIdType.MESH
CONTRACT_LAST = (((1,), (1,)), ((), ()))

X_ORDER = (2, 1, 3)
NEAR = (0, 1, 7, 2, 6, 3, 5, 4)
GROUPS = ((0, 5), (5, 8))
SLOTS = 24
X_BLOCKS = X_ORDER + (0,)
Y_ORDER = (2, 1, 3)
Z_ORDER = (4, 3, 5, 2, 6, 1, 7)
Z_ARRIVAL = (4, 3, 5, 2, 6, 1, 7)
PLANE = sorted(
    ((dy, dx) for dy in range(4) for dx in range(4) if (dy, dx) != (0, 0)),
    key=lambda p: -(min(p[0], 4 - p[0]) + min(p[1], 4 - p[1])),
)
OWNERS = (
    (2, 2), (2, 1), (1, 2), (2, 3), (3, 2), (2, 0), (0, 2),
    (1, 1), (1, 3), (3, 1), (1, 0), (0, 1), (3, 3), (3, 0), (0, 3), (0, 0),
)
COL = [(dx, dh) for dx in (2, 1, 3) for dh in (1, 0)] + [(0, 1)]


def dot(a, b):
    return jnp.dot(a, b, preferred_element_type=F32)


def dot_last(a, b):
    return lax.dot_general(a, b, CONTRACT_LAST, preferred_element_type=F32)


def kernel(
    rhs_ref, root_ref, fwd_ref, coup_ref, rinv_ref, back_ref, bwd_ref, rows_ref,
    both_ref,
    rhs_v, fwd_v, coup_v, rinv_v, back_v, bwd_v, root_v, rows_v,
    part_f, part_b, core_in, x_f, x_out, x_in, rs_in, ag, y_keep,
    u_f, u_b, u_in, u_all, place, pick, p_rhs,
    xp_f, xp_b, xp_in, xr_all, rb_all, sel_out, sel_in, sel_all,
    z_out, a_f, b_f, a_in, b_in, a_out, b_out, fa_in, fb_in, own_f, own_in, flip, flip2,
    load_sem, send_sem, core_r, rs_r, xs_r, ag_r, pr_r, w_r, us_r, za_r, ya_r, xc_r, xo_r, rb_r, se_r, pl_r,
    fa_r, fb_r, end_r,
):
    l, r, q = lax.axis_index("leaf"), lax.axis_index("row"), lax.axis_index("col")
    x, h = q // 2, q % 2
    sib = (l, r, x * 2 + 1 - h)

    def xat(d):
        return lax.rem(x + d, 4)

    def yat(d):
        return lax.rem(r + d, 4)

    def zat(d):
        return lax.rem(l + d, 8)

    def load(src, dst, k):
        c = pltpu.make_async_copy(src, dst, load_sem.at[k])
        c.start()
        return c

    pending = []
    count = [0]

    def send(src, dst, rs, device):
        if len(pending) == SLOTS:
            pending.pop(0).wait_send()
        c = pltpu.make_async_remote_copy(
            src_ref=src, dst_ref=dst, send_sem=send_sem.at[count[0] % SLOTS], recv_sem=rs, device_id=device, device_id_type=MESH
        )
        c.start()
        count[0] += 1
        pending.append(c)

    def arrive(dst, rs):
        pltpu.make_async_remote_copy(
            src_ref=dst, dst_ref=dst, send_sem=send_sem.at[0], recv_sem=rs, device_id=sib, device_id_type=MESH
        ).wait_recv()

    def flush():
        while pending:
            pending.pop(0).wait_send()

    partners = [(l, r, xat(dx) * 2 + lax.rem(h + dh, 2)) for dx, dh in COL]
    partners += [(l, yat(dy), xat(dx) * 2 + h) for dy, dx in PLANE if dy]
    partners += [(l, yat(d), x * 2 + 1 - h) for d in Y_ORDER]
    partners += [(zat(d), r, q) for d in Z_ORDER[::-1]]
    bar = pltpu.get_barrier_semaphore()
    for p in partners[::-1]:
        pl.semaphore_signal(bar, inc=1, device_id=p, device_id_type=MESH)

    l_rhs = load(rhs_ref, rhs_v, 0)
    l_fwd = []
    for j, d in enumerate(X_BLOCKS):
        cols = pl.ds(pl.multiple_of(xat(d) * 384, 128), 384)
        l_fwd.append(load(fwd_ref.at[:, cols], fwd_v.at[j], 1 + j))
    l_coup = load(coup_ref, coup_v.at[h], 6)
    l_rows = load(rows_ref, rows_v.at[l], 5)

    l_rhs.wait()
    for j in range(4):
        l_fwd[j].wait()
        value = dot(rhs_v[...], fwd_v[j])
        part_f[j] = value
        part_b[j] = value.astype(BF)
        if j == 0:
            pl.semaphore_wait(bar, len(partners))
        for g in range(2):
            core = lax.rem(h + g, 2)
            if X_BLOCKS[j] or g:
                send(
                    part_b.at[j, pl.ds(pl.multiple_of(core * 64 + 32, 32), 32)], rs_in.at[min(2 * j + g, 6)], rs_r.at[0],
                    (l, r, xat(X_BLOCKS[j]) * 2 + core),
                )
        send(part_b.at[j, pl.ds(pl.multiple_of(64 - h * 64, 32), 32)], core_in.at[j], core_r.at[j], sib)
    l_root = [
        load(root_ref.at[pl.ds(pl.multiple_of(g * 64 + r * 16, 16), 16)], root_v.at[pl.ds(g * 16, 16)], 11 + g)
        for g in range(2)
    ]
    l_rinv = load(rinv_ref, rinv_v, 8)
    l_back = load(back_ref, back_v.at[h], 9)
    l_bwd = load(bwd_ref, bwd_v.at[h], 10)
    l_coup.wait()
    send(coup_v.at[h], coup_v.at[h], w_r.at[2], sib)
    for j, d in enumerate(X_BLOCKS):
        arrive(core_in.at[j], core_r.at[j])
        both = part_f[j, pl.ds(pl.multiple_of(h * 64, 32), 32), :] + core_in[j].astype(F32)
        x_f[j] = both
        x_out[j] = both.astype(BF)
        for i, e in enumerate(X_ORDER):
            block = xat(d)
            send(x_out.at[j], x_in.at[block, i], xs_r.at[block], (l, r, xat(e) * 2 + h))

    l_rows.wait()
    for d in Z_ORDER:
        send(rows_ref, rows_v.at[l], pr_r.at[0 if d in (1, 7, 2, 6) else 1], (zat(d), r, q))

    def build_place(leaf):
        row = rows_v[leaf, :, pl.ds(pl.multiple_of(q * 512, 512), 512)] - q * 1536

        @pl.loop(0, 12)
        def _(t):
            at = lax.broadcasted_iota(jnp.int32, (128, 512), 0) + t * 128
            place[leaf, pl.ds(pl.multiple_of(t * 128, 128), 128), :] = (at == row).astype(F32).astype(BF)

    def build_pick(leaf):
        row = rows_v[leaf, :, pl.ds(pl.multiple_of(l * 512 + r * 128, 128), 128)] - l * 1536

        @pl.loop(0, 12)
        def _(t):
            at = lax.broadcasted_iota(jnp.int32, (128, 128), 0) + t * 128
            pick[leaf, pl.ds(pl.multiple_of(t * 128, 128), 128), :] = (at == row).astype(F32).astype(BF)

    build_place(l)

    total = part_f[3, pl.ds(pl.multiple_of(h * 64 + 32, 32), 32), :]
    arrive(rs_in, rs_r.at[0])
    for i in range(7):
        total = total + rs_in[i].astype(F32)
    y_keep[32:64, :] = total
    ag[x] = total.astype(BF)
    for i, e in enumerate(X_ORDER):
        send(ag.at[x], ag.at[x], ag_r.at[i], (l, r, xat(e) * 2 + h))
    arrive(rows_v.at[0:4], pr_r.at[0])
    for d in (1, 7, 2, 6):
        build_place(zat(d))

    arrive(coup_v.at[1 - h], w_r.at[2])
    update = [jnp.zeros((64, 512), F32) for _ in range(2)]
    for d in (0, 1, 3, 2):
        block = xat(d)
        total = x_f[X_BLOCKS.index(d)]
        arrive(x_in.at[block], xs_r.at[block])
        for i in range(3):
            total = total + x_in[block, i].astype(F32)
        if d:
            i = X_ORDER.index((4 - d) % 4)
            arrive(ag.at[block], ag_r.at[i])
        else:
            y_keep[0:32, :] = total
        left = jnp.concatenate([total.astype(BF), ag[block]], axis=0)
        rows = pl.ds(pl.multiple_of(block * 384, 128), 384)
        for g in range(2):
            core = lax.rem(h + g, 2)
            update[g] = update[g] + dot(left, coup_v[core, rows, :])
            if d == 2:
                u_b[g] = update[g].astype(BF)
                for i, e in enumerate(Y_ORDER + ((0,) if g else ())):
                    k = pl.ds(pl.multiple_of(yat(e) * 16, 16), 16)
                    send(u_b.at[g, k], u_in.at[g, i], us_r.at[g], (l, yat(e), x * 2 + core))
    u_f[...] = update[0]

    l_back.wait()
    l_bwd.wait()
    send(back_v.at[h], back_v.at[h], w_r.at[0], sib)
    send(bwd_v.at[h], bwd_v.at[h], w_r.at[1], sib)
    arrive(rows_v.at[0:3], pr_r.at[1])
    for d in (3, 5, 4):
        build_place(zat(d))
    total = u_f[pl.ds(pl.multiple_of(r * 16, 16), 16), :]
    arrive(u_in.at[0, 0:3], us_r.at[0])
    for i in range(3):
        total = total + u_in[0, i].astype(F32)
    half = pl.ds(pl.multiple_of(h * 16, 16), 16)
    u_all[l, half, :] = total.astype(BF)
    for j, d in enumerate(Z_ORDER):
        send(u_all.at[l, half], u_all.at[l, half], za_r.at[j], (zat(d), r, q))
    total = jnp.zeros((16, 512), F32)
    arrive(u_in.at[1], us_r.at[1])
    for i in range(4):
        total = total + u_in[1, i].astype(F32)
    half = pl.ds(pl.multiple_of((1 - h) * 16, 16), 16)
    u_all[l, half, :] = total.astype(BF)

    for j, d in enumerate(Z_ORDER):
        send(u_all.at[l, half], u_all.at[l, half], za_r.at[j], (zat(d), r, q))
    for c in l_root:
        c.wait()
    placed = root_v[...] - dot_last(u_all[l], place[l])
    for d in Z_ARRIVAL[:6]:
        j = Z_ORDER.index((8 - d) % 8)
        leaf = zat(d)
        arrive(u_all.at[leaf], za_r.at[j])
        placed = placed - dot_last(u_all[leaf], place[leaf])
    d = Z_ARRIVAL[6]
    leaf = zat(d)
    arrive(u_all.at[leaf], za_r.at[Z_ORDER.index((8 - d) % 8)])

    for t in range(3):
        cols = slice(t * 512, t * 512 + 512)
        p_rhs[t, r] = (placed[:, cols] - dot_last(u_all[leaf], place[leaf, cols, :])).astype(BF)
        for i, d in enumerate(Y_ORDER):
            send(p_rhs.at[t, r], p_rhs.at[t, r], ya_r.at[t], (l, yat(d), q))
    for d in range(8):
        build_pick(zat(d))
    l_rinv.wait()
    value = jnp.zeros((128, 384), F32)
    for t in range(3):
        arrive(p_rhs.at[t, 0:3], ya_r.at[t])
        value = value + dot(p_rhs[t].reshape(128, 512), rinv_v[pl.ds(t * 512, 512), :])

    xp_f[...] = value
    xp_b[...] = value.astype(BF)
    for j, (dx, dh) in enumerate(COL):
        tx, th = xat(dx), lax.rem(h + dh, 2)
        k = pl.ds(pl.multiple_of(tx * 32 + th * 16, 16), 16)
        send(xp_b.at[k], xp_in.at[j], xc_r.at[0], (l, r, tx * 2 + th))
    own_k = pl.ds(pl.multiple_of(h * 64 + x * 16, 16), 16)
    total = xp_f[pl.ds(pl.multiple_of(x * 32 + h * 16, 16), 16), :]
    arrive(xp_in, xc_r.at[0])
    for j in range(7):
        total = total + xp_in[j].astype(F32)
    rb_all[r] = total.astype(BF)

    for d in Y_ORDER:
        send(rb_all.at[r], rb_all.at[r], rb_r.at[0], (l, yat(d), q))
    xr_all[own_k, :] = total
    for j, (dx, dh) in enumerate(COL):
        send(xr_all.at[own_k], xr_all.at[own_k], xo_r.at[0], (l, r, xat(dx) * 2 + lax.rem(h + dh, 2)))
    arrive(rb_all.at[0:3], rb_r.at[0])
    root_rows = jnp.concatenate([rb_all[t] for t in range(4)], axis=1)

    for d in Z_ORDER + (0,):
        child = zat(d)
        chosen = dot(root_rows, pick[child]).astype(BF)
        if d:
            n = NEAR.index(8 - d)
            sel_out[child] = chosen
            send(sel_out.at[child], sel_in.at[n], se_r.at[0 if n < GROUPS[0][1] else 1], (child, r, q))
        else:
            sel_in[0] = chosen
    arrive(xr_all.at[0:112], xo_r.at[0])
    flip[...] = xr_all[...].T
    both_ref[0:48, :] = flip[pl.ds(pl.multiple_of(q * 48, 16), 48), :]

    for g, (low, high) in enumerate(GROUPS):
        arrive(sel_in.at[max(low, 1) : high], se_r.at[g])
        for dy, dx in PLANE:
            send(
                sel_in.at[low:high], sel_all.at[r, x, low:high], pl_r.at[g, dy], (l, yat(dy), xat(dx) * 2 + h)
            )
        sel_all[r, x, low:high] = sel_in[low:high]
    arrive(back_v.at[1 - h], w_r.at[0])
    arrive(bwd_v.at[1 - h], w_r.at[1])
    corr = jnp.zeros((64, 384), F32)
    for g, (low, high) in enumerate(GROUPS):
        for dy in (0, 1, 3, 2):
            sr = yat(dy)
            arrive(sel_all.at[sr, 0 : 4 if dy else 3, low:high], pl_r.at[g, (4 - dy) % 4])
            left = jnp.concatenate([sel_all[sr, :, n].reshape(64, 128) for n in range(low, high)], axis=1)
            right = jnp.concatenate(
                [
                    back_v[:, :, pl.ds(pl.multiple_of(zat(NEAR[n]) * 512 + sr * 128, 128), 128)].reshape(384, 128)
                    for n in range(low, high)
                ],
                axis=1,
            )
            corr = corr + dot_last(left, right)
    reduced = (y_keep[...] - corr).astype(BF)

    for j, (dy, dx) in enumerate(OWNERS):
        cols = pl.ds(pl.multiple_of((yat(dy) * 4 + xat(dx)) * 384, 128), 384)
        value = dot(reduced, bwd_v[:, :, cols].reshape(384, 384))
        z_out[j] = value.astype(BF)
        if dx:
            send(z_out.at[j, 0:32], a_in.at[dy, dx - 1], core_r.at[dy], (l, r, xat(dx) * 2 + h))
        else:
            a_f[dy] = value[0:32]
        if dy:
            send(z_out.at[j, 32:64], b_in.at[dx, dy - 1], xs_r.at[dx], (l, yat(dy), x * 2 + h))
        else:
            b_f[dx] = value[32:64]
    for c in pending[:-24]:
        c.wait_send()
    del pending[:-24]
    for d in (2, 1, 3, 0):
        for first, came, came_r, on, fin, fin_r, at in (
            (a_f, a_in, core_r, a_out, fa_in, fa_r, 0), (b_f, b_in, xs_r, b_out, fb_in, fb_r, 32)
        ):
            total = first[d]
            arrive(came.at[d], came_r.at[d])
            for i in range(3):
                total = total + came[d, i].astype(F32)
            if d:
                on[d - 1] = total.astype(BF)
                for g in range(2):
                    to = (l, r, xat(d) * 2 + g) if at else (l, yat(d), x * 2 + g)
                    send(on.at[d - 1, :, g * 128 : g * 128 + 256], fin.at[d - 1, h], fin_r.at[d - 1], to)
            else:
                own_f[at : at + 32, :] = total

    send(
        own_f.at[:, pl.ds(pl.multiple_of((1 - h) * 128, 128), 256)], own_in.at[h], end_r.at[0], sib
    )
    own_in[h] = own_f[:, pl.ds(pl.multiple_of(h * 128, 128), 256)]
    flush()
    arrive(own_in.at[1 - h], end_r.at[0])
    for d in (2, 1, 3):
        for fin, fin_r, at in ((fa_in, fa_r, 0), (fb_in, fb_r, 32)):
            arrive(fin.at[d - 1], fin_r.at[d - 1])
            for c in range(2):
                own_in[c, at : at + 32] = own_in[c, at : at + 32] + fin[d - 1, c].astype(F32)
    flip2[...] = own_in[...].reshape(128, 256).T
    both_ref[48:240, :] = flip2[pl.ds(pl.multiple_of(h * 64, 64), 192), :]


def split(both_ref, xroot_ref, xchild_ref):
    xroot_ref[...] = both_ref[0:48, :]
    xchild_ref[...] = both_ref[48:240, :]


def local(
    rhs_child, rhs_root, fwd_child, coupling, root_inverse, back_child, bwd_child, parent_rows
):
    vm = pltpu.VMEM
    dma = pltpu.SemaphoreType.DMA
    scratch = [
        vm((128, 768), BF), vm((4, 768, 384), BF), vm((2, 1536, 512), BF), vm((1536, 384), BF),
        vm((2, 192, 4096), BF), vm((2, 192, 6144), BF), vm((32, 1536), F32), vm((8, 1, 4096), jnp.int32),
        vm((4, 128, 384), F32), vm((4, 128, 384), BF), vm((4, 32, 384), BF), vm((4, 32, 384), F32),
        vm((4, 32, 384), BF), vm((4, 3, 32, 384), BF), vm((7, 32, 384), BF), vm((4, 32, 384), BF), vm((64, 384), F32),
        vm((64, 512), F32), vm((2, 64, 512), BF), vm((2, 4, 16, 512), BF), vm((8, 32, 512), BF),
        vm((8, 1536, 512), BF), vm((8, 1536, 128), BF), vm((3, 4, 32, 512), BF),
        vm((128, 384), F32), vm((128, 384), BF), vm((7, 16, 384), BF), vm((128, 384), F32),
        vm((4, 16, 384), BF), vm((8, 16, 128), BF), vm((8, 16, 128), BF), vm((4, 4, 8, 16, 128), BF),
        vm((16, 64, 384), BF), vm((4, 32, 384), F32), vm((4, 32, 384), F32),
        vm((4, 3, 32, 384), BF), vm((4, 3, 32, 384), BF), vm((3, 32, 384), BF), vm((3, 32, 384), BF),
        vm((3, 2, 32, 256), BF), vm((3, 2, 32, 256), BF), vm((64, 384), F32), vm((2, 64, 256), F32),
        vm((384, 128), F32), vm((256, 128), F32),
        dma((13,)), dma((SLOTS,)),
    ]
    for n in (4, 1, 4, 3, 2, 3, 2, 7, 3, 1, 1, 1, 2, (2, 4), 3, 3, 1):
        scratch.append(dma(n if isinstance(n, tuple) else (n,)))
    any_spec = pl.BlockSpec(memory_space=pl.ANY)
    vm_spec = pl.BlockSpec(memory_space=pltpu.VMEM)
    both = pl.pallas_call(
        kernel,
        out_shape=pltpu.VMEM((240, 128), F32),
        in_specs=[any_spec] * 8,
        out_specs=vm_spec,
        scratch_shapes=scratch,
        compiler_params=pltpu.CompilerParams(
            collective_id=0, has_side_effects=True, vmem_limit_bytes=56 * 2**20
        ),
    )(
        rhs_child[0], rhs_root, fwd_child[0], coupling[0], root_inverse, back_child[0].T, bwd_child[0], parent_rows
    )
    x_root, x_child = pl.pallas_call(
        split,
        out_shape=(jax.ShapeDtypeStruct((48, 128), F32), jax.ShapeDtypeStruct((192, 128), F32)),
        in_specs=[vm_spec],
        out_specs=(vm_spec, vm_spec),
    )(pltpu.with_memory_space_constraint(both, pltpu.VMEM))
    return (x_root.T, x_child.T[None])


def solution(mesh):
    placed = (
        P("leaf", None, "col"),
        P(None, "col"),
        P("leaf", "col", "row"),
        P("leaf", "row", "col"),
        P("col", ("leaf", "row")),
        P("leaf", None, ("row", "col")),
        P("leaf", ("row", "col"), None),
        P("leaf", None),
    )
    return jax.shard_map(
        local,
        mesh=mesh,
        in_specs=placed,
        out_specs=(P(None, ("leaf", "row", "col")), P("leaf", None, ("row", "col"))),
        check_vma=False,
    )
```
